128 devices in a mesh: row: 32 (over z, y, x_hi), col: 4 (over x_lo, core).
Axes of the slice: x: 4 (x_hi: 2, x_lo: 2; x = x_hi * 2 + x_lo), y: 4, z: 4, core: 2. Of those that a mesh axis runs over, the one named last changes fastest.
Arguments:
- source: bfloat16 [64, 32768], P(None, ('row', 'col')), may hold values from -1 to 1
- target: bfloat16 [64, 98304], P(None, ('col', 'row')), may hold values from -1 to 1
- source_logw: float32 [32768], P('row'), may hold values from -3 to 0
- target_logw: float32 [98304], P(('col', 'row')), may hold values from -3 to 0
- start_potential: bfloat16 [1, 98304], P(None, ('col', 'row')), may hold values from -1 to 12
Outputs:
- row_potential: float32 [32768], P('row')
- col_potential: float32 [98304], P(('col', 'row'))
The draws below stay inside these ranges and needn't reach their ends.
All inputs are finite; a program needn't handle non-finite values.
Results may differ from the reference program's by a relative error of at most 0.0015.
Values may be sent and summed in bfloat16 or wider, within the bound.
No kernel may reach another device: no remote copies, remote signals or barrier semaphores. Data moves between devices by JAX's collectives and lax.ppermute only.
A program may use at most 64 MiB of HBM per device.

```python
import jax
import jax.numpy as jnp
from jax import lax

DIM = 64
SOURCES = 32768
TARGETS = 98304


def draw_source(key, part):
    key = jax.random.fold_in(key, 11)
    first = jax.random.fold_in(key, 0)
    return (jax.random.truncated_normal(first, -4.0, 4.0, (DIM, SOURCES), jnp.float32) * 0.25).astype(jnp.bfloat16)


def draw_target(key, part):
    key = jax.random.fold_in(key, 17)
    first = jax.random.fold_in(key, 0)
    return (jax.random.truncated_normal(first, -4.0, 4.0, (DIM, TARGETS), jnp.float32) * 0.25).astype(jnp.bfloat16)


def draw_start_potential(key, part):
    key = jax.random.fold_in(key, 29)
    first = jax.random.fold_in(key, 0)
    return (jax.random.truncated_normal(first, -4.0, 4.0, (1, TARGETS), jnp.float32) * 0.05).astype(jnp.bfloat16)


def shard_levels(own_key, shape, cuts, low, top_value):
    factor_of = 1.0
    for axis_at, blocks in cuts:
        steps = jax.random.uniform(jax.random.fold_in(jax.random.fold_in(own_key, 6), axis_at), (blocks,), jnp.float32, low / len(cuts), top_value / len(cuts))
        factor_of = factor_of * jnp.repeat(jnp.exp(steps), shape[axis_at] // blocks).reshape((-1,) + (1,) * (len(shape) - 1 - axis_at))
    return factor_of


def setup_inputs(seed: int = 0) -> dict:
    splits = jax.random.split(jax.random.key(seed), 6)
    return {
        "source": draw_source(jax.random.fold_in(splits[5], 71), 0),
        "target": draw_target(jax.random.fold_in(splits[5], 71), 0),
        "source_logw": jnp.clip(-3.0 + 3.0 * jax.random.uniform(splits[2], (SOURCES,), jnp.float32) ** shard_levels(splits[2], (SOURCES,), ((0, 32),), -0.2, 0.2), -3.0, 0.0),
        "target_logw": jnp.clip(-3.0 + 3.0 * jax.random.uniform(splits[3], (TARGETS,), jnp.float32) ** shard_levels(splits[3], (TARGETS,), ((0, 128),), -0.2, 0.2), -3.0, 0.0),
        "start_potential": draw_start_potential(jax.random.fold_in(splits[5], 71), 0),
    }


smoothing = 0.1


def column_norms(points):
    wide = points.astype(jnp.float32)
    return jnp.sum(wide * wide, axis=0)


def cost_block(rows, row_sq, cols, col_sq):
    inner = lax.dot_general(rows, cols, (((0,), (0,)), ((), ())), preferred_element_type=jnp.float32)
    return row_sq[:, None] + col_sq[None, :] - 2.0 * inner


def reference(source, target, source_logw, target_logw, start_potential):
    width = 512 if SOURCES % 512 == 0 else SOURCES
    blocks = SOURCES // width
    src_sq = column_norms(source)
    tgt_sq = column_norms(target)
    lifted = start_potential[0].astype(jnp.float32)
    src_blocks = source.reshape(DIM, blocks, width).transpose(1, 0, 2)
    sq_blocks = src_sq.reshape(blocks, width)

    def row_half(item):
        rows, row_sq = item
        scores = (lifted[None, :] - cost_block(rows, row_sq, target, tgt_sq)) / smoothing
        top = jnp.max(scores, axis=1)
        return top + jnp.log(jnp.sum(jnp.exp(scores - top[:, None]), axis=1))

    row_lse = lax.map(row_half, (src_blocks, sq_blocks)).reshape(SOURCES)
    row_potential = smoothing * source_logw - smoothing * row_lse
    pot_blocks = row_potential.reshape(blocks, width)

    def col_half(carry, item):
        col_top, col_sum = carry
        rows, row_sq, pots = item
        scores = (pots[:, None] - cost_block(rows, row_sq, target, tgt_sq)) / smoothing
        top = jnp.maximum(col_top, jnp.max(scores, axis=0))
        col_sum = col_sum * jnp.exp(col_top - top) + jnp.sum(jnp.exp(scores - top[None, :]), axis=0)
        return (top, col_sum), None

    start = (jnp.full((TARGETS,), -1e30, jnp.float32), jnp.zeros((TARGETS,), jnp.float32))
    (col_top, col_sum), _ = lax.scan(col_half, start, (src_blocks, sq_blocks, pot_blocks))
    col_potential = smoothing * target_logw - smoothing * (col_top + jnp.log(col_sum))
    return (row_potential, col_potential)
```

```python
import functools
import math

import jax
import jax.numpy as jnp
from jax import lax
from jax.experimental import pallas as pl
from jax.experimental.pallas import tpu as pltpu
from jax.sharding import Mesh
from jax.sharding import PartitionSpec as P

smoothing = 0.1
log2e = math.log2(math.e)
kappa = 2.0 * log2e / smoothing
scale = log2e / smoothing
dim = 64
headroom = 56.0
largest = 3e38
shape = (4, 4, 2, 2, 2)
names = ("z", "y", "xh", "xl", "core")


def three_parts(x):
    hi = x.astype(jnp.bfloat16).astype(jnp.float32)
    mid = (x - hi).astype(jnp.bfloat16).astype(jnp.float32)
    return hi, mid, x - hi - mid


def streamed_features(points, bias):
    m = points.shape[1]
    hi, mid, lo = three_parts(bias)
    row = lax.broadcasted_iota(jnp.int32, (16, m), 0)
    extra = jnp.where(row == 0, hi, jnp.where(row == 1, mid, jnp.where(row == 2, lo, 0.0)))
    extra = jnp.where(row == 3, 1.0, extra).astype(jnp.bfloat16)
    block = jnp.concatenate([points, extra, jnp.zeros((48, m), jnp.bfloat16)], axis=0)
    return block.T


def held_features(points, shift):
    n = points.shape[1]
    wide = points.astype(jnp.float32) * kappa
    hi = wide.astype(jnp.bfloat16)
    lo = (wide - hi.astype(jnp.float32)).astype(jnp.bfloat16)
    row = lax.broadcasted_iota(jnp.int32, (16, n), 0)
    extra = jnp.where(row < 3, 1.0, jnp.where(row == 3, -shift, 0.0)).astype(jnp.bfloat16)
    return jnp.concatenate(
        [hi, extra, jnp.zeros((48, n), jnp.bfloat16), lo, jnp.zeros((64, n), jnp.bfloat16)], axis=0
    )


def scores(stream_ref, start, size, held):
    u = stream_ref[pl.ds(start, size), :]
    return lax.dot_general(
        jnp.concatenate([u, u], axis=1),
        held,
        (((1,), (0,)), ((), ())),
        preferred_element_type=jnp.float32,
    )


def log_sums(stream_ref, points, chunk, unroll, sample=128):
    m, n = stream_ref.shape[0], points.shape[1]

    def start_of(c):
        return pl.multiple_of(c * chunk, chunk)

    def total(shift):
        held = held_features(points, shift)

        def step(c, acc):
            e = jnp.exp2(scores(stream_ref, start_of(c), chunk, held))
            return acc + jnp.sum(e.reshape(chunk // 8, 8, n), axis=0)

        acc = lax.fori_loop(0, m // chunk, step, jnp.zeros((8, n), jnp.float32), unroll=unroll)
        return jnp.sum(acc, axis=0, keepdims=True)

    def rounded(x):
        return x.astype(jnp.bfloat16).astype(jnp.float32)

    bare = held_features(points, jnp.zeros((1, n), jnp.float32))
    top = jnp.max(scores(stream_ref, 0, sample, bare), axis=0, keepdims=True)
    shift = rounded(top + headroom)
    sums = total(shift)

    def again():
        def step(c, acc):
            x = scores(stream_ref, start_of(c), chunk, bare)
            return jnp.maximum(acc, jnp.max(x, axis=0, keepdims=True))

        exact = rounded(lax.fori_loop(0, m // chunk, step, top))
        return exact + jnp.log2(total(exact))

    return lax.cond(jnp.max(sums) < largest, lambda: shift + jnp.log2(sums), again)


def row_kernel(t_ref, s_ref, out_ref, stream_ref):
    pieces, _, width = t_ref.shape

    @pl.when(pl.program_id(0) == 0)
    def _():
        for k in range(pieces):
            points = t_ref[k, :dim, :]
            lifted = t_ref[k, dim : dim + 1, :].astype(jnp.float32)
            wide = points.astype(jnp.float32)
            bias = scale * (lifted - jnp.sum(wide * wide, axis=0, keepdims=True))
            stream_ref[k * width : (k + 1) * width, :] = streamed_features(points, bias)

    points = jnp.concatenate([s_ref[k, :dim, :] for k in range(s_ref.shape[0])], axis=1)
    out_ref[...] = log_sums(stream_ref, points, 1024, 3)


def column_kernel(s_ref, lse_ref, t_ref, out_ref, stream_ref):
    pieces, _, width = s_ref.shape

    @pl.when(pl.program_id(0) == 0)
    def _():
        for k in range(pieces):
            logw = s_ref[k, dim : dim + 3, :].astype(jnp.float32)
            logw = jnp.sum(logw, axis=0, keepdims=True)
            bias = log2e * logw - lse_ref[:, k * width : (k + 1) * width]
            stream_ref[k * width : (k + 1) * width, :] = streamed_features(s_ref[k, :dim, :], bias)

    points = jnp.concatenate([t_ref[k, :dim, :] for k in range(t_ref.shape[0])], axis=1)
    out_ref[...] = log_sums(stream_ref, points, 1024, 2)


params = dict(
    compiler_params=pltpu.CompilerParams(vmem_limit_bytes=48 * 2**20),
)


def row_sums(targets, sources):
    pieces, height, width = targets.shape
    count, s_height, s_width = sources.shape
    take = 2
    return pl.pallas_call(
        row_kernel,
        grid=(count // take,),
        in_specs=[
            pl.BlockSpec((pieces, height, width), lambda i: (0, 0, 0)),
            pl.BlockSpec((take, s_height, s_width), lambda i: (i, 0, 0)),
        ],
        out_specs=pl.BlockSpec((1, take * s_width), lambda i: (0, i)),
        out_shape=jax.ShapeDtypeStruct((1, count * s_width), jnp.float32),
        scratch_shapes=[pltpu.VMEM((pieces * width, 128), jnp.bfloat16)],
        name="row_sums",
        **params,
    )(targets, sources)


def column_sums(sources, lse, targets):
    pieces, height, width = sources.shape
    count, t_height, t_width = targets.shape
    return pl.pallas_call(
        column_kernel,
        grid=(count,),
        in_specs=[
            pl.BlockSpec((pieces, height, width), lambda i: (0, 0, 0)),
            pl.BlockSpec((1, pieces * width), lambda i: (0, 0)),
            pl.BlockSpec((1, t_height, t_width), lambda i: (i, 0, 0)),
        ],
        out_specs=pl.BlockSpec((1, t_width), lambda i: (0, i)),
        out_shape=jax.ShapeDtypeStruct((1, count * t_width), jnp.float32),
        scratch_shapes=[pltpu.VMEM((pieces * width, 128), jnp.bfloat16)],
        name="column_sums",
        **params,
    )(sources, lse, targets)


def exchange(x, axes, flip):
    size = lax.axis_size(axes)
    return lax.ppermute(x, axes, [(i, i ^ flip) for i in range(size)])


def doubled(x, axes, flip, bit):
    other = exchange(x, axes, flip)
    first = bit == 0
    return jnp.concatenate([jnp.where(first, x, other), jnp.where(first, other, x)], axis=0)


def log_add(a, b):
    top = jnp.maximum(a, b)
    return top + jnp.log2(1.0 + jnp.exp2(-jnp.abs(a - b)))


def norms(points):
    wide = points.astype(jnp.float32)
    return jnp.sum(wide * wide, axis=0)


def per_device(source, target, source_logw, target_logw, start_potential):
    z, y, xh, xl, core = (lax.axis_index(name) for name in names)
    width, span = source.shape[1], target.shape[1]
    own = lax.dynamic_slice_in_dim(source_logw, (2 * xl + core) * width, width, 0)
    first = lax.reduce_precision(own, 8, 7)
    second = lax.reduce_precision(own - first, 8, 7)
    parts = jnp.stack([first, second, own - first - second]).astype(jnp.bfloat16)
    sources = jnp.concatenate([source, parts], axis=0)[None]
    targets = jnp.concatenate([target, start_potential], axis=0)[None]
    x = ("xh", "xl")

    sources = doubled(sources, x, 1, xl)
    targets = doubled(targets, x, 3, xh)
    sources = doubled(sources, "z", 1, z % 2)
    targets = doubled(targets, "y", 1, y % 2)
    sources = doubled(sources, "z", 3, z // 2)
    targets = doubled(targets, "y", 3, y // 2)
    sources = doubled(sources, "core", 1, core)

    lse = row_sums(targets, sources)
    for axes, flip in (("core", 1), (x, 1), ("z", 1), ("z", 3)):
        lse = log_add(lse, exchange(lse, axes, flip))

    partial = column_sums(sources, lse, targets).reshape(2, 2, 2, span)
    for axes, flip, bit in (("y", 3, y // 2), ("y", 1, y % 2), (x, 3, xh)):
        kept = lax.dynamic_index_in_dim(partial, bit, 0, False)
        sent = lax.dynamic_index_in_dim(partial, 1 - bit, 0, False)
        partial = log_add(kept, exchange(sent, axes, flip))

    mine = lax.dynamic_index_in_dim(lse.reshape(2, 4, 2, width), z, 1, False)
    mine = mine.transpose(1, 0, 2).reshape(4 * width)
    picked = lax.dynamic_index_in_dim(
        sources[:, :dim, :].reshape(2, 4, 2, dim, width), z, 1, False
    )
    row_sq = jnp.sum(jnp.square(picked.astype(jnp.float32)), axis=2)
    row_sq = row_sq.transpose(1, 0, 2).reshape(4 * width)
    row_lse = mine / log2e - row_sq / smoothing
    row_potential = smoothing * source_logw - smoothing * row_lse

    col_lse = partial / log2e - norms(target) / smoothing
    col_potential = smoothing * target_logw - smoothing * col_lse
    return (row_potential, col_potential)


def solution(mesh):
    devices = Mesh(mesh.devices.reshape(shape), names)
    rows = ("z", "y", "xh")
    columns = ("xl", "core", "z", "y", "xh")
    in_specs = (P(None, names), P(None, columns), P(rows), P(columns), P(None, columns))
    out_specs = (P(rows), P(columns))
    return jax.shard_map(
        per_device, mesh=devices, in_specs=in_specs, out_specs=out_specs, check_vma=False
    )
```

```python
import functools
import math

import jax
import jax.numpy as jnp
from jax import lax
from jax.experimental import pallas as pl
from jax.experimental.pallas import tpu as pltpu
from jax.sharding import Mesh
from jax.sharding import PartitionSpec as P

smoothing = 0.1
log2e = math.log2(math.e)
kappa = 2.0 * log2e / smoothing
scale = log2e / smoothing
dim = 64
headroom = 24.0
sample = 128
row_blocks = (1024, 1024, 1)
column_blocks = (1024, 1024, 1)
largest = 3e38
shape = (4, 4, 2, 2, 2)
names = ("z", "y", "xh", "xl", "core")


def three_parts(x):
    hi = x.astype(jnp.bfloat16).astype(jnp.float32)
    mid = (x - hi).astype(jnp.bfloat16).astype(jnp.float32)
    return hi, mid, x - hi - mid


def streamed_features(points, bias):
    m = points.shape[1]
    hi, mid, lo = three_parts(bias)
    row = lax.broadcasted_iota(jnp.int32, (16, m), 0)
    extra = jnp.where(row == 0, hi, jnp.where(row == 1, mid, jnp.where(row == 2, lo, 0.0)))
    extra = jnp.where(row == 3, 1.0, extra).astype(jnp.bfloat16)
    block = jnp.concatenate([points, extra, jnp.zeros((48, m), jnp.bfloat16)], axis=0)
    return block.T


def held_extra(shift):
    row = lax.broadcasted_iota(jnp.int32, (16, shift.shape[1]), 0)
    return jnp.where(row < 3, 1.0, jnp.where(row == 3, -shift, 0.0)).astype(jnp.bfloat16)


def fill_held(held_ref, start, points):
    n = points.shape[1]
    cols = slice(start, start + n)
    wide = points.astype(jnp.float32) * kappa
    hi = wide.astype(jnp.bfloat16)
    held_ref[:dim, cols] = hi
    held_ref[dim + 16 : 2 * dim, cols] = jnp.zeros((dim - 16, n), jnp.bfloat16)
    held_ref[2 * dim : 3 * dim, cols] = (wide - hi.astype(jnp.float32)).astype(jnp.bfloat16)
    held_ref[3 * dim :, cols] = jnp.zeros((dim, n), jnp.bfloat16)


def rounded(x):
    return x.astype(jnp.bfloat16).astype(jnp.float32)


def log_sums(stream_ref, held_ref, out_ref, shift_ref, prior, chunk, tile, unroll):
    m, n = stream_ref.shape[0], held_ref.shape[1]
    extra = slice(dim, dim + 16)

    def scores(start, size, cols):
        u = stream_ref[pl.ds(start, size), :]
        return lax.dot_general(
            jnp.concatenate([u, u], axis=1),
            held_ref[:, cols],
            (((1,), (0,)), ((), ())),
            preferred_element_type=jnp.float32,
        )

    def tiles(step, unroll=1):
        def body(t, _):
            step(pl.ds(pl.multiple_of(t * tile, tile), tile))
            return 0

        lax.fori_loop(0, n // tile, body, 0, unroll=unroll)

    def shift_by(shift):
        shift_ref[...] = shift
        held_ref[extra, :] = held_extra(shift)

    def add_up(cols):
        acc = jnp.zeros((8, tile), jnp.float32)
        for c in range(m // chunk):
            e = jnp.exp2(scores(c * chunk, chunk, cols))
            acc = acc + jnp.sum(e.reshape(chunk // 8, 8, tile), axis=0)
        out_ref[:, cols] = jnp.sum(acc, axis=0, keepdims=True)

    def sums():
        tiles(add_up, unroll)
        if prior is None:
            return out_ref[...]
        return out_ref[...] + jnp.exp2(prior - shift_ref[...])

    if prior is None:
        held_ref[extra, :] = held_extra(jnp.zeros((1, n), jnp.float32))
        top = jnp.max(scores(0, sample, slice(None)), axis=0, keepdims=True)
    else:
        top = prior
    shift_by(rounded(top + headroom))
    total = sums()
    out_ref[...] = shift_ref[...] + jnp.log2(total)

    @pl.when(jnp.logical_not(jnp.max(total) < largest))
    def _():
        held_ref[extra, :] = held_extra(jnp.zeros((1, n), jnp.float32))

        def exact(cols):
            def step(c, acc):
                x = scores(pl.multiple_of(c * chunk, chunk), chunk, cols)
                return jnp.maximum(acc, jnp.max(x, axis=0, keepdims=True))

            out_ref[:, cols] = lax.fori_loop(
                0, m // chunk, step, jnp.full((1, tile), -largest, jnp.float32)
            )

        tiles(exact)
        highest = out_ref[...] if prior is None else jnp.maximum(out_ref[...], prior)
        shift_by(rounded(highest))
        total = sums()
        out_ref[...] = shift_ref[...] + jnp.log2(total)


def fill_row_stream(t_ref, stream_ref):
    pieces, _, width = t_ref.shape
    for k in range(pieces):
        points = t_ref[k, :dim, :]
        lifted = t_ref[k, dim : dim + 1, :].astype(jnp.float32)
        wide = points.astype(jnp.float32)
        bias = scale * (lifted - jnp.sum(wide * wide, axis=0, keepdims=True))
        stream_ref[k * width : (k + 1) * width, :] = streamed_features(points, bias)


def row_kernel(t_ref, s_ref, *refs):
    prior_ref, (out_ref, stream_ref, held_ref, shift_ref) = refs[:-4], refs[-4:]
    fill_row_stream(t_ref, stream_ref)
    for k in range(s_ref.shape[0]):
        fill_held(held_ref, k * s_ref.shape[2], s_ref[k, :dim, :])
    prior = prior_ref[0][...] if prior_ref else None
    log_sums(stream_ref, held_ref, out_ref, shift_ref, prior, *row_blocks)


def column_kernel(s_ref, lse_ref, t_ref, out_ref, stream_ref, held_ref, shift_ref):
    pieces, _, width = s_ref.shape
    for k in range(pieces):
        logw = s_ref[k, dim : dim + 3, :].astype(jnp.float32)
        logw = jnp.sum(logw, axis=0, keepdims=True)
        bias = log2e * logw - lse_ref[:, k * width : (k + 1) * width]
        stream_ref[k * width : (k + 1) * width, :] = streamed_features(s_ref[k, :dim, :], bias)
    for k in range(t_ref.shape[0]):
        fill_held(held_ref, k * t_ref.shape[2], t_ref[k, :dim, :])
    log_sums(stream_ref, held_ref, out_ref, shift_ref, None, *column_blocks)


def call(kernel, name, m, n, *operands):
    whole = pl.BlockSpec(memory_space=pltpu.VMEM)
    return pl.pallas_call(
        kernel,
        in_specs=[whole] * len(operands),
        out_specs=whole,
        out_shape=jax.ShapeDtypeStruct((1, n), jnp.float32),
        scratch_shapes=[
            pltpu.VMEM((m, 128), jnp.bfloat16),
            pltpu.VMEM((256, n), jnp.bfloat16),
            pltpu.VMEM((1, n), jnp.float32),
        ],
        compiler_params=pltpu.CompilerParams(vmem_limit_bytes=40 * 2**20),
        name=name,
    )(*operands)


def row_sums(targets, sources, *prior):
    m = targets.shape[0] * targets.shape[2]
    n = sources.shape[0] * sources.shape[2]
    return call(row_kernel, "row_sums", m, n, targets, sources, *prior)


def column_sums(sources, lse, targets):
    m = sources.shape[0] * sources.shape[2]
    n = targets.shape[0] * targets.shape[2]
    return call(column_kernel, "column_sums", m, n, sources, lse, targets)


def exchange(x, axes, flip):
    size = lax.axis_size(axes)
    return lax.ppermute(x, axes, [(i, i ^ flip) for i in range(size)])


def doubled(x, axes, flip, bit):
    other = exchange(x, axes, flip)
    first = bit == 0
    return jnp.concatenate([jnp.where(first, x, other), jnp.where(first, other, x)], axis=0)


def log_add(a, b):
    top = jnp.maximum(a, b)
    return top + jnp.log2(1.0 + jnp.exp2(-jnp.abs(a - b)))


def norms(points):
    wide = points.astype(jnp.float32)
    return jnp.sum(wide * wide, axis=0)


def per_device(source, target, source_logw, target_logw, start_potential):
    z, y, xh, xl, core = (lax.axis_index(name) for name in names)
    width, span = source.shape[1], target.shape[1]
    own = lax.dynamic_slice_in_dim(source_logw, (2 * xl + core) * width, width, 0)
    first = lax.reduce_precision(own, 8, 7)
    second = lax.reduce_precision(own - first, 8, 7)
    parts = jnp.stack([first, second, own - first - second]).astype(jnp.bfloat16)
    sources = jnp.concatenate([source, parts], axis=0)[None]
    targets = jnp.concatenate([target, start_potential], axis=0)[None]
    x = ("xh", "xl")

    sources = doubled(sources, x, 1, xl)
    targets = jnp.concatenate([targets, exchange(targets, x, 3)], axis=0)
    sources = doubled(sources, "z", 1, z % 2)
    targets = jnp.concatenate([targets, exchange(targets, "y", 1)], axis=0)
    sources = doubled(sources, "z", 3, z // 2)
    sources = doubled(sources, "core", 1, core)
    others = exchange(targets, "y", 3)

    lse = row_sums(others, sources, row_sums(targets, sources))
    for axes, flip in (("core", 1), (x, 1), ("z", 1), ("z", 3)):
        lse = log_add(lse, exchange(lse, axes, flip))

    sent = exchange(column_sums(sources, lse, others), "y", 3)
    partial = log_add(column_sums(sources, lse, targets), sent).reshape(2, 2, span)
    partial = log_add(partial[0], exchange(partial[1], "y", 1))
    partial = log_add(partial[0], exchange(partial[1], x, 3))

    mine = lax.dynamic_index_in_dim(lse.reshape(2, 4, 2, width), z, 1, False)
    mine = mine.transpose(1, 0, 2).reshape(4 * width)
    picked = lax.dynamic_index_in_dim(
        sources[:, :dim, :].reshape(2, 4, 2, dim, width), z, 1, False
    )
    row_sq = jnp.sum(jnp.square(picked.astype(jnp.float32)), axis=2)
    row_sq = row_sq.transpose(1, 0, 2).reshape(4 * width)
    row_lse = mine / log2e - row_sq / smoothing
    row_potential = smoothing * source_logw - smoothing * row_lse

    col_lse = partial / log2e - norms(target) / smoothing
    col_potential = smoothing * target_logw - smoothing * col_lse
    return (row_potential, col_potential)


def solution(mesh):
    devices = Mesh(mesh.devices.reshape(shape), names)
    rows = ("z", "y", "xh")
    columns = ("xl", "core", "z", "y", "xh")
    in_specs = (P(None, names), P(None, columns), P(rows), P(columns), P(None, columns))
    out_specs = (P(rows), P(columns))
    return jax.shard_map(
        per_device, mesh=devices, in_specs=in_specs, out_specs=out_specs, check_vma=False
    )
```

```python
import functools
import math

import jax
import jax.numpy as jnp
from jax import lax
from jax.experimental import pallas as pl
from jax.experimental.pallas import tpu as pltpu
from jax.sharding import Mesh
from jax.sharding import PartitionSpec as P

smoothing = 0.1
log2e = math.log2(math.e)
kappa = 2.0 * log2e / smoothing
scale = log2e / smoothing
dim = 64
headroom = 24.0
sample = 128
row_blocks = (1024, 1024)
column_blocks = (1024, 768)
largest = 3e38
shape = (4, 4, 2, 2, 2)
names = ("z", "y", "xh", "xl", "core")
x = ("xh", "xl")


def three_parts(v):
    hi = v.astype(jnp.bfloat16).astype(jnp.float32)
    mid = (v - hi).astype(jnp.bfloat16).astype(jnp.float32)
    return hi, mid, v - hi - mid


def rounded(v):
    return v.astype(jnp.bfloat16).astype(jnp.float32)


def log_add(a, b):
    top = jnp.maximum(a, b)
    return top + jnp.log2(1.0 + jnp.exp2(-jnp.abs(a - b)))


def streamed_features(points, bias):
    m = points.shape[1]
    hi, mid, lo = three_parts(bias)
    row = lax.broadcasted_iota(jnp.int32, (16, m), 0)
    extra = jnp.where(row == 0, hi, jnp.where(row == 1, mid, jnp.where(row == 2, lo, 0.0)))
    extra = jnp.where(row == 3, 1.0, extra).astype(jnp.bfloat16)
    block = jnp.concatenate([points, extra, jnp.zeros((48, m), jnp.bfloat16)], axis=0)
    return block.T


def fill_held(held_ref, start, points):
    cols = slice(start, start + points.shape[1])
    wide = points.astype(jnp.float32) * kappa
    hi = wide.astype(jnp.bfloat16)
    held_ref[:dim, cols] = hi
    held_ref[dim:, cols] = (wide - hi.astype(jnp.float32)).astype(jnp.bfloat16)


class LogSums:
    def __init__(self, stream_ref, held_ref, extra_ref, out_ref, shift_ref, blocks):
        self.stream_ref, self.held_ref, self.extra_ref = stream_ref, held_ref, extra_ref
        self.out_ref, self.shift_ref = out_ref, shift_ref
        self.chunk, self.tile = blocks
        self.m, self.n = stream_ref.shape[0], held_ref.shape[1]

    def scores(self, start, size, cols):
        u = self.stream_ref[pl.ds(start, size), :]
        held = self.held_ref[:, cols]
        zeros = jnp.zeros((dim, held.shape[1]), jnp.bfloat16)
        held = jnp.concatenate(
            [held[:dim], self.extra_ref[:, cols], zeros[:48], held[dim:], zeros], axis=0
        )
        return lax.dot_general(
            jnp.concatenate([u, u], axis=1),
            held,
            (((1,), (0,)), ((), ())),
            preferred_element_type=jnp.float32,
        )

    def set_extra(self, shift):
        row = lax.broadcasted_iota(jnp.int32, (16, self.n), 0)
        extra = jnp.where(row < 3, 1.0, jnp.where(row == 3, -shift, 0.0))
        self.extra_ref[...] = extra.astype(jnp.bfloat16)

    def tiles(self, step):
        def body(t, _):
            step(pl.ds(pl.multiple_of(t * self.tile, self.tile), self.tile))
            return 0

        lax.fori_loop(0, self.n // self.tile, body, 0)

    def estimate(self):
        self.set_extra(jnp.zeros((1, self.n), jnp.float32))
        top = jnp.max(self.scores(0, sample, slice(None)), axis=0, keepdims=True)
        self.shift_ref[...] = rounded(top + headroom)

    def sums(self):
        self.set_extra(self.shift_ref[...])

        def add_up(cols):
            acc = jnp.zeros((8, self.tile), jnp.float32)
            for c in range(self.m // self.chunk):
                e = jnp.exp2(self.scores(c * self.chunk, self.chunk, cols))
                acc = acc + jnp.sum(e.reshape(self.chunk // 8, 8, self.tile), axis=0)
            self.out_ref[:, cols] = jnp.sum(acc, axis=0, keepdims=True)

        self.tiles(add_up)
        return self.out_ref[...]

    def exact(self):
        self.set_extra(jnp.zeros((1, self.n), jnp.float32))

        def highest(cols):
            def step(c, acc):
                start = pl.multiple_of(c * self.chunk, self.chunk)
                v = self.scores(start, self.chunk, cols)
                return jnp.maximum(acc, jnp.max(v, axis=0, keepdims=True))

            none = jnp.full((1, self.tile), -largest, jnp.float32)
            self.out_ref[:, cols] = lax.fori_loop(0, self.m // self.chunk, step, none)

        self.tiles(highest)
        return self.out_ref[...]

    def run(self, prior=None):
        if prior is None:
            self.estimate()

        def total():
            s = self.sums()
            return s if prior is None else s + jnp.exp2(prior - self.shift_ref[...])

        s = total()
        self.out_ref[...] = self.shift_ref[...] + jnp.log2(s)

        @pl.when(jnp.logical_not(jnp.max(s) < largest))
        def _():
            top = self.exact()
            self.shift_ref[...] = rounded(top if prior is None else jnp.maximum(top, prior))
            s = total()
            self.out_ref[...] = self.shift_ref[...] + jnp.log2(s)


def fill_row_stream(t_ref, stream_ref):
    width = t_ref.shape[1]
    pieces = t_ref.shape[0] // (dim + 1)
    for k in range(pieces):
        points = t_ref[k * dim : (k + 1) * dim, :]
        lifted = t_ref[pieces * dim + k : pieces * dim + k + 1, :].astype(jnp.float32)
        wide = points.astype(jnp.float32)
        bias = scale * (lifted - jnp.sum(wide * wide, axis=0, keepdims=True))
        stream_ref[k * width : (k + 1) * width, :] = streamed_features(points, bias)


def rows(s_ref, stream_ref, out_ref, held_ref, shift_ref, extra_ref):
    for k in range(s_ref.shape[0]):
        fill_held(held_ref, k * s_ref.shape[2], s_ref[k])
    LogSums(stream_ref, held_ref, extra_ref, out_ref, shift_ref, row_blocks).run()


def first_row_kernel(t_ref, s_ref, stream_ref, out_ref, held_ref, shift_ref, extra_ref):
    fill_row_stream(t_ref, stream_ref)
    rows(s_ref, stream_ref, out_ref, held_ref, shift_ref, extra_ref)


def second_row_kernel(stream_ref, s_ref, out_ref, held_ref, shift_ref, extra_ref):
    rows(s_ref, stream_ref, out_ref, held_ref, shift_ref, extra_ref)


def last_row_kernel(t_ref, *refs):
    ins, outs = refs[:6], refs[6:8]
    stream_ref, extra_ref, shift_ref = refs[8:]
    fill_row_stream(t_ref, stream_ref)
    for half, out_ref in enumerate(outs):
        prior_ref, held_ref, old_ref = ins[3 * half : 3 * half + 3]
        shift_ref[...] = old_ref[...]
        sums = LogSums(stream_ref, held_ref, extra_ref, out_ref, shift_ref, row_blocks)
        sums.run(prior_ref[...])


def fill_column_stream(s_refs, lse_ref, received_ref, logw_ref, place_ref, stream_ref):
    per, _, width = s_refs[0].shape
    n = lse_ref.shape[1]
    half = logw_ref.shape[1]
    here, there = logw_ref[...], received_ref[:, n:]
    ordered = place_ref[0] == 0
    logw = (jnp.where(ordered, here, there), jnp.where(ordered, there, here))
    first = place_ref[1] == 0
    for k in range(2 * per):
        other, hi, lo, xl = k // 8, k // 4 % 2, k // 2 % 2, k % 2
        at = lo * (half // 2) + 2 * xl * width
        mass = [logw[hi][:, at + c * width : at + (c + 1) * width] for c in (other, 1 - other)]
        mass = jnp.where(first, mass[0], mass[1])
        cols = slice(k * width, (k + 1) * width)
        lse = log_add(lse_ref[:, cols], received_ref[:, cols])
        bias = log2e * mass - lse
        stream_ref[cols, :] = streamed_features(s_refs[other][k % per], bias)


def columns(first, t_ref, out_ref, stream_ref, held_ref, extra_ref, shift_ref):
    width = t_ref.shape[1]
    for k in range(held_ref.shape[1] // width):
        points = t_ref[(first + k) * dim : (first + k + 1) * dim, :]
        fill_held(held_ref, k * width, points)
    LogSums(stream_ref, held_ref, extra_ref, out_ref, shift_ref, column_blocks).run()


def first_column_kernel(
    a_ref, b_ref, lse_ref, received_ref, logw_ref, place_ref, t_ref, out_ref, stream_ref, *scratch
):
    fill_column_stream((a_ref, b_ref), lse_ref, received_ref, logw_ref, place_ref, stream_ref)
    columns(0, t_ref, out_ref, stream_ref, *scratch)


def next_column_kernel(first, stream_ref, t_ref, out_ref, *scratch):
    columns(first, t_ref, out_ref, stream_ref, *scratch)


whole = pl.BlockSpec(memory_space=pltpu.VMEM)
scalar = pl.BlockSpec(memory_space=pltpu.SMEM)


def call(kernel, name, operands, outs, scratch, in_specs=None):
    return pl.pallas_call(
        kernel,
        in_specs=in_specs or [whole] * len(operands),
        out_specs=[whole] * len(outs),
        out_shape=[jax.ShapeDtypeStruct(*o) for o in outs],
        scratch_shapes=[pltpu.VMEM(*s) for s in scratch],
        compiler_params=pltpu.CompilerParams(vmem_limit_bytes=40 * 2**20),
        name=name,
    )(*operands)


def stream_of(points):
    return ((points, 128), jnp.bfloat16)


def arrays_of(n):
    row = ((1, n), jnp.float32)
    return row, ((2 * dim, n), jnp.bfloat16), ((16, n), jnp.bfloat16)


def points_of(targets):
    return targets.shape[0] // (dim + 1) * targets.shape[1]


def first_row_sums(targets, sources):
    row, held, extra = arrays_of(sources.shape[0] * sources.shape[2])
    outs = (stream_of(points_of(targets)), row, held, row)
    return call(first_row_kernel, "first_row_sums", (targets, sources), outs, (extra,))


def second_row_sums(stream, sources):
    row, held, extra = arrays_of(sources.shape[0] * sources.shape[2])
    outs = (row, held, row)
    return call(second_row_kernel, "second_row_sums", (stream, sources), outs, (extra,))


def last_row_sums(targets, a, b):
    row, _, extra = arrays_of(a[0].shape[1])
    scratch = (stream_of(points_of(targets)), extra, row)
    return call(last_row_kernel, "last_row_sums", (targets, *a, *b), (row, row), scratch)


def first_column_sums(sources, lse, received, logw, place, targets):
    row, held, extra = arrays_of(points_of(targets))
    return call(
        first_column_kernel,
        "first_column_sums",
        (*sources, lse, received, logw, place, targets),
        (row, stream_of(lse.shape[1])),
        (held, extra, row),
        [whole] * 5 + [scalar, whole],
    )


def next_column_sums(stream, targets, first, count):
    row, held, extra = arrays_of(count * targets.shape[1])
    kernel = functools.partial(next_column_kernel, first)
    return call(kernel, "next_column_sums", (stream, targets), (row,), (held, extra, row))[0]


def exchange(v, axes, flip):
    size = lax.axis_size(axes)
    return lax.ppermute(v, axes, [(i, i ^ flip) for i in range(size)])


def in_order(bit, v, other):
    first = bit == 0
    return jnp.concatenate([jnp.where(first, v, other), jnp.where(first, other, v)], axis=0)


def doubled(v, axes, flip, bit):
    return in_order(bit, v, exchange(v, axes, flip))


def with_more(targets, more):
    a, b = (v.shape[0] // (dim + 1) * dim for v in (targets, more))
    return jnp.concatenate([targets[:a], more[:b], targets[a:], more[b:]], axis=0)


def norms(points):
    wide = points.astype(jnp.float32)
    return jnp.sum(wide * wide, axis=0)


def per_device(source, target, source_logw, target_logw, start_potential):
    z, y, xh, xl, core = (lax.axis_index(name) for name in names)
    width, span = source.shape[1], target.shape[1]
    place = jnp.stack([z // 2, core]).astype(jnp.int32)

    yx = ("y", "xh", "xl")
    targets = jnp.concatenate([target, start_potential], axis=0)
    own = doubled(source[None], x, 1, xl)
    along_y = exchange(targets, "y", 1)
    along_xx = exchange(targets, x, 3)
    both_t = exchange(targets, yx, 7)
    own = doubled(own, "z", 1, z % 2)
    own, along_y, along_xx, both_t = lax.optimization_barrier((own, along_y, along_xx, both_t))
    targets = with_more(with_more(targets, along_y), with_more(along_xx, both_t))
    others = exchange(targets, "y", 3)
    own = doubled(own, "z", 3, z // 2)
    other = exchange(own, "core", 1)

    stream, *a = first_row_sums(targets, own)
    b = second_row_sums(stream, other)
    lse = jnp.concatenate(last_row_sums(others, a, b), axis=1)
    count = lse.shape[1]
    received = exchange(lse, "core", 1)
    swapped = jnp.concatenate([received[:, count // 2 :], received[:, : count // 2]], axis=1)
    lse = log_add(lse, swapped)
    lse = log_add(lse, exchange(lse, x, 1))
    logw = source_logw[None]
    received = exchange(jnp.concatenate([lse, logw], axis=1), "z", 1)
    lse = log_add(lse, received[:, :count])
    first = z % 2 == 0
    received = received[:, count:]
    logw = jnp.concatenate(
        [jnp.where(first, logw, received), jnp.where(first, received, logw)], axis=1
    )
    received = exchange(jnp.concatenate([lse, logw], axis=1), "z", 3)

    partial, stream = first_column_sums((own, other), lse, received, logw, place, others)
    sent = exchange(partial, "y", 3)
    half = 2 * span
    partial = next_column_sums(stream, targets, 2, 2)
    partial = log_add(partial, sent[:, half:])
    sent = log_add(exchange(partial, x, 3), sent[:, :half])
    partial = log_add(next_column_sums(stream, targets, 0, 2), sent)[0]
    partial = log_add(partial[:span], exchange(partial[span:], "y", 1))

    lse = log_add(lse, received[:, :count])
    mine = lax.dynamic_index_in_dim(lse.reshape(2, 4, 2, width), z, 1, False)
    picked = [lax.dynamic_index_in_dim(s.reshape(4, 2, dim, width), z, 0, False) for s in (own, other)]
    row_sq = jnp.stack([jnp.sum(jnp.square(p.astype(jnp.float32)), axis=1) for p in picked])
    row_lse = mine / log2e - row_sq / smoothing
    row_lse = jnp.where(core == 0, row_lse, row_lse[::-1])
    row_lse = row_lse.transpose(1, 0, 2).reshape(4 * width)
    row_potential = smoothing * source_logw - smoothing * row_lse

    col_lse = partial / log2e - norms(target) / smoothing
    col_potential = smoothing * target_logw - smoothing * col_lse
    return (row_potential, col_potential)


def solution(mesh):
    devices = Mesh(mesh.devices.reshape(shape), names)
    rows = ("z", "y", "xh")
    columns_over = ("xl", "core", "z", "y", "xh")
    in_specs = (P(None, names), P(None, columns_over), P(rows), P(columns_over), P(None, columns_over))
    out_specs = (P(rows), P(columns_over))
    return jax.shard_map(
        per_device, mesh=devices, in_specs=in_specs, out_specs=out_specs, check_vma=False
    )
```

```python
import functools
import math

import jax
import jax.numpy as jnp
from jax import lax
from jax.experimental import pallas as pl
from jax.experimental.pallas import tpu as pltpu
from jax.sharding import Mesh
from jax.sharding import PartitionSpec as P

smoothing = 0.1
log2e = math.log2(math.e)
kappa = 2.0 * log2e / smoothing
scale = log2e / smoothing
dim = 64
headroom = 24.0
sample = 128
row_blocks = (1024, 1024)
column_blocks = (1024, 768)
largest = 3e38
shape = (4, 4, 2, 2, 2)
names = ("z", "y", "xh", "xl", "core")
x = ("xh", "xl")


def three_parts(v):
    hi = v.astype(jnp.bfloat16).astype(jnp.float32)
    mid = (v - hi).astype(jnp.bfloat16).astype(jnp.float32)
    return hi, mid, v - hi - mid


def rounded(v):
    return v.astype(jnp.bfloat16).astype(jnp.float32)


def log_add(a, b):
    top = jnp.maximum(a, b)
    return top + jnp.log2(1.0 + jnp.exp2(-jnp.abs(a - b)))


def streamed_features(points, bias):
    m = points.shape[1]
    hi, mid, lo = three_parts(bias)
    row = lax.broadcasted_iota(jnp.int32, (16, m), 0)
    extra = jnp.where(row == 0, hi, jnp.where(row == 1, mid, jnp.where(row == 2, lo, 0.0)))
    extra = jnp.where(row == 3, 1.0, extra).astype(jnp.bfloat16)
    block = jnp.concatenate([points, extra, jnp.zeros((48, m), jnp.bfloat16)], axis=0)
    return block.T


def fill_held(held_ref, start, points):
    cols = slice(start, start + points.shape[1])
    wide = points.astype(jnp.float32) * kappa
    hi = wide.astype(jnp.bfloat16)
    held_ref[:dim, cols] = hi
    held_ref[dim:, cols] = (wide - hi.astype(jnp.float32)).astype(jnp.bfloat16)


class LogSums:
    def __init__(self, stream_ref, held_ref, extra_ref, out_ref, shift_ref, blocks):
        self.stream_ref, self.held_ref, self.extra_ref = stream_ref, held_ref, extra_ref
        self.out_ref, self.shift_ref = out_ref, shift_ref
        self.chunk, self.tile = blocks
        self.m, self.n = stream_ref.shape[0], held_ref.shape[1]

    def scores(self, start, size, cols):
        u = self.stream_ref[pl.ds(start, size), :]
        held = self.held_ref[:, cols]
        zeros = jnp.zeros((dim, held.shape[1]), jnp.bfloat16)
        held = jnp.concatenate(
            [held[:dim], self.extra_ref[:, cols], zeros[:48], held[dim:], zeros], axis=0
        )
        return lax.dot_general(
            jnp.concatenate([u, u], axis=1),
            held,
            (((1,), (0,)), ((), ())),
            preferred_element_type=jnp.float32,
        )

    def set_extra(self, shift):
        row = lax.broadcasted_iota(jnp.int32, (16, self.n), 0)
        extra = jnp.where(row < 3, 1.0, jnp.where(row == 3, -shift, 0.0))
        self.extra_ref[...] = extra.astype(jnp.bfloat16)

    def tiles(self, step):
        def body(t, _):
            step(pl.ds(pl.multiple_of(t * self.tile, self.tile), self.tile))
            return 0

        lax.fori_loop(0, self.n // self.tile, body, 0)

    def estimate(self):
        self.set_extra(jnp.zeros((1, self.n), jnp.float32))
        top = jnp.max(self.scores(0, sample, slice(None)), axis=0, keepdims=True)
        self.shift_ref[...] = rounded(top + headroom)

    def sums(self):
        self.set_extra(self.shift_ref[...])

        def add_up(cols):
            acc = jnp.zeros((8, self.tile), jnp.float32)
            for c in range(self.m // self.chunk):
                e = jnp.exp2(self.scores(c * self.chunk, self.chunk, cols))
                acc = acc + jnp.sum(e.reshape(self.chunk // 8, 8, self.tile), axis=0)
            self.out_ref[:, cols] = jnp.sum(acc, axis=0, keepdims=True)

        self.tiles(add_up)
        return self.out_ref[...]

    def exact(self):
        self.set_extra(jnp.zeros((1, self.n), jnp.float32))

        def highest(cols):
            def step(c, acc):
                v = self.scores(pl.multiple_of(c * sample, sample), sample, cols)
                return jnp.maximum(acc, jnp.max(v, axis=0, keepdims=True))

            none = jnp.full((1, self.tile), -largest, jnp.float32)
            self.out_ref[:, cols] = lax.fori_loop(0, self.m // sample, step, none)

        self.tiles(highest)
        return self.out_ref[...]

    def run(self, prior=None):
        if prior is None:
            self.estimate()

        def attempt(state):
            total = self.sums()
            if prior is not None:
                total = total + jnp.exp2(prior - self.shift_ref[...])
            again = jnp.logical_not(jnp.max(total) < largest)
            self.out_ref[...] = self.shift_ref[...] + jnp.log2(total)

            @pl.when(again)
            def _():
                top = self.exact()
                self.shift_ref[...] = rounded(top if prior is None else jnp.maximum(top, prior))

            return state[0] + 1, again

        lax.while_loop(lambda s: jnp.logical_and(s[1], s[0] < 2), attempt, (0, True))


def fill_row_stream(t_ref, stream_ref):
    pieces, _, width = t_ref.shape
    for k in range(pieces):
        points = t_ref[k, :dim, :]
        lifted = t_ref[k, dim : dim + 1, :].astype(jnp.float32)
        wide = points.astype(jnp.float32)
        bias = scale * (lifted - jnp.sum(wide * wide, axis=0, keepdims=True))
        stream_ref[k * width : (k + 1) * width, :] = streamed_features(points, bias)


def first_row_kernel(t_ref, s_ref, out_ref, held_ref, shift_ref, stream_ref, extra_ref):
    fill_row_stream(t_ref, stream_ref)
    for k in range(s_ref.shape[0]):
        fill_held(held_ref, k * s_ref.shape[2], s_ref[k, :dim, :])
    LogSums(stream_ref, held_ref, extra_ref, out_ref, shift_ref, row_blocks).run()


def next_row_kernel(t_ref, held_ref, old_ref, prior_ref, out_ref, stream_ref, extra_ref, shift_ref):
    fill_row_stream(t_ref, stream_ref)
    shift_ref[...] = old_ref[...]
    LogSums(stream_ref, held_ref, extra_ref, out_ref, shift_ref, row_blocks).run(prior_ref[...])


def fill_column_stream(s_ref, lse_ref, received_ref, logw_ref, place_ref, stream_ref):
    pieces, _, width = s_ref.shape
    n = lse_ref.shape[1]
    half = logw_ref.shape[1]
    here, there = logw_ref[...], received_ref[:, n:]
    ordered = place_ref[0] == 0
    logw = (jnp.where(ordered, here, there), jnp.where(ordered, there, here))
    for k in range(pieces):
        core, hi, lo, xl = k // 8, k // 4 % 2, k // 2 % 2, k % 2
        at = lo * (half // 2) + (2 * xl + core) * width
        cols = slice(k * width, (k + 1) * width)
        lse = log_add(lse_ref[:, cols], received_ref[:, cols])
        bias = log2e * logw[hi][:, at : at + width] - lse
        stream_ref[cols, :] = streamed_features(s_ref[k], bias)


def columns(first, t_ref, out_ref, stream_ref, held_ref, extra_ref, shift_ref):
    width = t_ref.shape[2]
    for k in range(held_ref.shape[1] // width):
        fill_held(held_ref, k * width, t_ref[first + k, :dim, :])
    LogSums(stream_ref, held_ref, extra_ref, out_ref, shift_ref, column_blocks).run()


def first_column_kernel(*refs):
    ins, (t_ref, out_ref, stream_ref), scratch = refs[:-6], refs[-6:-3], refs[-3:]
    fill_column_stream(*ins, stream_ref)
    columns(0, t_ref, out_ref, stream_ref, *scratch)


def next_column_kernel(first, stream_ref, t_ref, out_ref, *scratch):
    columns(first, t_ref, out_ref, stream_ref, *scratch)


whole = pl.BlockSpec(memory_space=pltpu.VMEM)
scalar = pl.BlockSpec(memory_space=pltpu.SMEM)


def call(kernel, name, operands, outs, scratch, in_specs=None):
    return pl.pallas_call(
        kernel,
        in_specs=in_specs or [whole] * len(operands),
        out_specs=[whole] * len(outs),
        out_shape=[jax.ShapeDtypeStruct(*o) for o in outs],
        scratch_shapes=[pltpu.VMEM(*s) for s in scratch],
        compiler_params=pltpu.CompilerParams(vmem_limit_bytes=40 * 2**20),
        name=name,
    )(*operands)


def stream_of(points):
    return ((points, 128), jnp.bfloat16)


def arrays_of(n):
    row = ((1, n), jnp.float32)
    return row, ((2 * dim, n), jnp.bfloat16), ((16, n), jnp.bfloat16)


def points_of(targets):
    return targets.shape[0] * targets.shape[2]


def first_row_sums(targets, sources):
    row, held, extra = arrays_of(points_of(sources))
    outs = (row, held, row)
    scratch = (stream_of(points_of(targets)), extra)
    return call(first_row_kernel, "first_row_sums", (targets, sources), outs, scratch)


def next_row_sums(targets, prior, held, shift):
    row, _, extra = arrays_of(held.shape[1])
    scratch = (stream_of(points_of(targets)), extra, row)
    return call(next_row_kernel, "next_row_sums", (targets, held, shift, prior), (row,), scratch)[0]


def first_column_sums(targets, sources, *more):
    row, held, extra = arrays_of(points_of(targets))
    operands = (sources, *more, targets)
    specs = [scalar if v.dtype == jnp.int32 else whole for v in operands]
    outs = (row, stream_of(points_of(sources)))
    return call(first_column_kernel, "first_column_sums", operands, outs, (held, extra, row), specs)


def next_column_sums(stream, targets, first, count):
    row, held, extra = arrays_of(count * targets.shape[2])
    kernel = functools.partial(next_column_kernel, first)
    return call(kernel, "next_column_sums", (stream, targets), (row,), (held, extra, row))[0]


def exchange(v, axes, flip):
    size = lax.axis_size(axes)
    return lax.ppermute(v, axes, [(i, i ^ flip) for i in range(size)])


def in_order(bit, v, other):
    first = bit == 0
    return jnp.concatenate([jnp.where(first, v, other), jnp.where(first, other, v)], axis=0)


def doubled(v, axes, flip, bit):
    return in_order(bit, v, exchange(v, axes, flip))


def norms(points):
    wide = points.astype(jnp.float32)
    return jnp.sum(wide * wide, axis=0)


def per_device(source, target, source_logw, target_logw, start_potential):
    z, y, xh, xl, core = (lax.axis_index(name) for name in names)
    width, span = source.shape[1], target.shape[1]

    sources = source[None]
    targets = jnp.concatenate([target, start_potential], axis=0)[None]
    sources = doubled(sources, x, 1, xl)
    targets = jnp.concatenate([targets, exchange(targets, x, 3)], axis=0)
    sources = doubled(sources, "z", 1, z % 2)
    targets = jnp.concatenate([targets, exchange(targets, "y", 1)], axis=0)
    sources = doubled(sources, "z", 3, z // 2)
    sources = doubled(sources, "core", 1, core)
    others = exchange(targets, "y", 3)

    lse, held, shift = first_row_sums(targets, sources)
    lse = next_row_sums(others, lse, held, shift)
    lse = log_add(lse, exchange(lse, "core", 1))
    lse = log_add(lse, exchange(lse, x, 1))
    count = lse.shape[1]
    logw = source_logw[None]
    received = exchange(jnp.concatenate([lse, logw], axis=1), "z", 1)
    lse = log_add(lse, received[:, :count])
    received = received[:, count:]
    logw = jnp.where(z % 2 == 0, jnp.concatenate([logw, received], axis=1), jnp.concatenate([received, logw], axis=1))
    received = exchange(jnp.concatenate([lse, logw], axis=1), "z", 3)
    place = (z // 2).astype(jnp.int32).reshape(1)
    partial, stream = first_column_sums(others, sources, lse, received, logw, place)

    sent = exchange(partial, "y", 3)
    half = 2 * span
    partial = next_column_sums(stream, targets, 2, 2)
    partial = log_add(partial, sent[:, half:])
    sent = log_add(exchange(partial, "y", 1), sent[:, :half])
    partial = log_add(next_column_sums(stream, targets, 0, 2), sent)[0]
    partial = log_add(partial[:span], exchange(partial[span:], x, 3))

    lse = log_add(lse, received[:, : lse.shape[1]])
    mine = lax.dynamic_index_in_dim(lse.reshape(2, 4, 2, width), z, 1, False)
    mine = mine.transpose(1, 0, 2).reshape(4 * width)
    picked = sources[:, :dim, :].reshape(2, 4, 2, dim, width)
    picked = lax.dynamic_index_in_dim(picked, z, 1, False)
    row_sq = jnp.sum(jnp.square(picked.astype(jnp.float32)), axis=2)
    row_sq = row_sq.transpose(1, 0, 2).reshape(4 * width)
    row_lse = mine / log2e - row_sq / smoothing
    row_potential = smoothing * source_logw - smoothing * row_lse

    col_lse = partial / log2e - norms(target) / smoothing
    col_potential = smoothing * target_logw - smoothing * col_lse
    return (row_potential, col_potential)


def solution(mesh):
    devices = Mesh(mesh.devices.reshape(shape), names)
    rows = ("z", "y", "xh")
    columns_over = ("xl", "core", "z", "y", "xh")
    in_specs = (P(None, names), P(None, columns_over), P(rows), P(columns_over), P(None, columns_over))
    out_specs = (P(rows), P(columns_over))
    return jax.shard_map(
        per_device, mesh=devices, in_specs=in_specs, out_specs=out_specs, check_vma=False
    )
```

```python
import functools
import math

import jax
import jax.numpy as jnp
from jax import lax
from jax.experimental import pallas as pl
from jax.experimental.pallas import tpu as pltpu
from jax.sharding import Mesh
from jax.sharding import PartitionSpec as P

smoothing = 0.1
log2e = math.log2(math.e)
kappa = 2.0 * log2e / smoothing
scale = log2e / smoothing
dim = 64
headroom = 24.0
sample = 128
row_blocks = (1024, 1024)
column_blocks = (1024, 768)
largest = 3e38
shape = (4, 4, 2, 2, 2)
names = ("z", "y", "xh", "xl", "core")
x = ("xh", "xl")


def three_parts(v):
    hi = v.astype(jnp.bfloat16).astype(jnp.float32)
    mid = (v - hi).astype(jnp.bfloat16).astype(jnp.float32)
    return hi, mid, v - hi - mid


def rounded(v):
    return v.astype(jnp.bfloat16).astype(jnp.float32)


def log_add(a, b):
    top = jnp.maximum(a, b)
    return top + jnp.log2(1.0 + jnp.exp2(-jnp.abs(a - b)))


def streamed_features(points, bias):
    m = points.shape[1]
    hi, mid, lo = three_parts(bias)
    row = lax.broadcasted_iota(jnp.int32, (16, m), 0)
    extra = jnp.where(row == 0, hi, jnp.where(row == 1, mid, jnp.where(row == 2, lo, 0.0)))
    extra = jnp.where(row == 3, 1.0, extra).astype(jnp.bfloat16)
    block = jnp.concatenate([points, extra, jnp.zeros((48, m), jnp.bfloat16)], axis=0)
    return block.T


def fill_held(held_ref, start, points):
    cols = slice(start, start + points.shape[1])
    wide = points.astype(jnp.float32) * kappa
    hi = wide.astype(jnp.bfloat16)
    held_ref[:dim, cols] = hi
    held_ref[dim:, cols] = (wide - hi.astype(jnp.float32)).astype(jnp.bfloat16)


class LogSums:
    def __init__(self, stream_ref, held_ref, extra_ref, out_ref, shift_ref, blocks):
        self.stream_ref, self.held_ref, self.extra_ref = stream_ref, held_ref, extra_ref
        self.out_ref, self.shift_ref = out_ref, shift_ref
        self.chunk, self.tile = blocks
        self.m, self.n = stream_ref.shape[0], held_ref.shape[1]
        self.unroll = 2 if self.n // self.tile % 2 == 0 and self.n > 2000 else 1

    def scores(self, start, size, cols):
        u = self.stream_ref[pl.ds(start, size), :]
        held = self.held_ref[:, cols]
        zeros = jnp.zeros((dim, held.shape[1]), jnp.bfloat16)
        held = jnp.concatenate(
            [held[:dim], self.extra_ref[:, cols], zeros[:48], held[dim:], zeros], axis=0
        )
        return lax.dot_general(
            jnp.concatenate([u, u], axis=1),
            held,
            (((1,), (0,)), ((), ())),
            preferred_element_type=jnp.float32,
        )

    def set_extra(self, shift):
        row = lax.broadcasted_iota(jnp.int32, (16, self.n), 0)
        extra = jnp.where(row < 3, 1.0, jnp.where(row == 3, -shift, 0.0))
        self.extra_ref[...] = extra.astype(jnp.bfloat16)

    def tiles(self, step):
        def body(t, _):
            step(pl.ds(pl.multiple_of(t * self.tile, self.tile), self.tile))
            return 0

        lax.fori_loop(0, self.n // self.tile, body, 0, unroll=self.unroll)

    def estimate(self):
        self.set_extra(jnp.zeros((1, self.n), jnp.float32))
        top = jnp.max(self.scores(0, sample, slice(None)), axis=0, keepdims=True)
        self.shift_ref[...] = rounded(top + headroom)

    def sums(self):
        self.set_extra(self.shift_ref[...])

        def add_up(cols):
            acc = jnp.zeros((8, self.tile), jnp.float32)
            for c in range(self.m // self.chunk):
                e = jnp.exp2(self.scores(c * self.chunk, self.chunk, cols))
                acc = acc + jnp.sum(e.reshape(self.chunk // 8, 8, self.tile), axis=0)
            self.out_ref[:, cols] = jnp.sum(acc, axis=0, keepdims=True)

        self.tiles(add_up)
        return self.out_ref[...]

    def exact(self):
        self.set_extra(jnp.zeros((1, self.n), jnp.float32))

        def highest(cols):
            def step(c, acc):
                v = self.scores(pl.multiple_of(c * sample, sample), sample, cols)
                return jnp.maximum(acc, jnp.max(v, axis=0, keepdims=True))

            none = jnp.full((1, self.tile), -largest, jnp.float32)
            self.out_ref[:, cols] = lax.fori_loop(0, self.m // sample, step, none)

        self.tiles(highest)
        return self.out_ref[...]

    def run(self, prior=None):
        if prior is None:
            self.estimate()

        def attempt(state):
            total = self.sums()
            if prior is not None:
                total = total + jnp.exp2(prior - self.shift_ref[...])
            again = jnp.logical_not(jnp.max(total) < largest)
            self.out_ref[...] = self.shift_ref[...] + jnp.log2(total)

            @pl.when(again)
            def _():
                top = self.exact()
                self.shift_ref[...] = rounded(top if prior is None else jnp.maximum(top, prior))

            return state[0] + 1, again

        lax.while_loop(lambda s: jnp.logical_and(s[1], s[0] < 2), attempt, (0, True))


def fill_row_stream(t_ref, stream_ref):
    pieces, _, width = t_ref.shape
    for k in range(pieces):
        points = t_ref[k, :dim, :]
        lifted = t_ref[k, dim : dim + 1, :].astype(jnp.float32)
        wide = points.astype(jnp.float32)
        bias = scale * (lifted - jnp.sum(wide * wide, axis=0, keepdims=True))
        stream_ref[k * width : (k + 1) * width, :] = streamed_features(points, bias)


def first_row_kernel(t_ref, s_ref, out_ref, held_ref, shift_ref, stream_ref, extra_ref):
    fill_row_stream(t_ref, stream_ref)
    for k in range(s_ref.shape[0]):
        fill_held(held_ref, k * s_ref.shape[2], s_ref[k, :dim, :])
    LogSums(stream_ref, held_ref, extra_ref, out_ref, shift_ref, row_blocks).run()


def next_row_kernel(t_ref, held_ref, old_ref, prior_ref, out_ref, stream_ref, extra_ref, shift_ref):
    fill_row_stream(t_ref, stream_ref)
    shift_ref[...] = old_ref[...]
    LogSums(stream_ref, held_ref, extra_ref, out_ref, shift_ref, row_blocks).run(prior_ref[...])


def fill_column_stream(s_ref, lse_ref, received_ref, logw_ref, place_ref, stream_ref):
    pieces, _, width = s_ref.shape
    n = lse_ref.shape[1]
    half = logw_ref.shape[1]
    here, there = logw_ref[...], received_ref[:, n:]
    ordered = place_ref[0] == 0
    logw = (jnp.where(ordered, here, there), jnp.where(ordered, there, here))
    for k in range(pieces):
        core, hi, lo, xl = k // 8, k // 4 % 2, k // 2 % 2, k % 2
        at = lo * (half // 2) + (2 * xl + core) * width
        cols = slice(k * width, (k + 1) * width)
        lse = log_add(lse_ref[:, cols], received_ref[:, cols])
        bias = log2e * logw[hi][:, at : at + width] - lse
        stream_ref[cols, :] = streamed_features(s_ref[k], bias)


def columns(first, t_ref, out_ref, stream_ref, held_ref, extra_ref, shift_ref):
    width = t_ref.shape[2]
    for k in range(held_ref.shape[1] // width):
        fill_held(held_ref, k * width, t_ref[first + k, :dim, :])
    LogSums(stream_ref, held_ref, extra_ref, out_ref, shift_ref, column_blocks).run()


def first_column_kernel(*refs):
    ins, (t_ref, out_ref, stream_ref), scratch = refs[:-6], refs[-6:-3], refs[-3:]
    fill_column_stream(*ins, stream_ref)
    columns(0, t_ref, out_ref, stream_ref, *scratch)


def next_column_kernel(first, stream_ref, t_ref, out_ref, *scratch):
    columns(first, t_ref, out_ref, stream_ref, *scratch)


whole = pl.BlockSpec(memory_space=pltpu.VMEM)
scalar = pl.BlockSpec(memory_space=pltpu.SMEM)


def call(kernel, name, operands, outs, scratch, in_specs=None):
    return pl.pallas_call(
        kernel,
        in_specs=in_specs or [whole] * len(operands),
        out_specs=[whole] * len(outs),
        out_shape=[jax.ShapeDtypeStruct(*o) for o in outs],
        scratch_shapes=[pltpu.VMEM(*s) for s in scratch],
        compiler_params=pltpu.CompilerParams(vmem_limit_bytes=40 * 2**20),
        name=name,
    )(*operands)


def stream_of(points):
    return ((points, 128), jnp.bfloat16)


def arrays_of(n):
    row = ((1, n), jnp.float32)
    return row, ((2 * dim, n), jnp.bfloat16), ((16, n), jnp.bfloat16)


def points_of(targets):
    return targets.shape[0] * targets.shape[2]


def first_row_sums(targets, sources):
    row, held, extra = arrays_of(points_of(sources))
    outs = (row, held, row)
    scratch = (stream_of(points_of(targets)), extra)
    return call(first_row_kernel, "first_row_sums", (targets, sources), outs, scratch)


def next_row_sums(targets, prior, held, shift):
    row, _, extra = arrays_of(held.shape[1])
    scratch = (stream_of(points_of(targets)), extra, row)
    return call(next_row_kernel, "next_row_sums", (targets, held, shift, prior), (row,), scratch)[0]


def first_column_sums(targets, sources, *more):
    row, held, extra = arrays_of(points_of(targets))
    operands = (sources, *more, targets)
    specs = [scalar if v.dtype == jnp.int32 else whole for v in operands]
    outs = (row, stream_of(points_of(sources)))
    return call(first_column_kernel, "first_column_sums", operands, outs, (held, extra, row), specs)


def next_column_sums(stream, targets, first, count):
    row, held, extra = arrays_of(count * targets.shape[2])
    kernel = functools.partial(next_column_kernel, first)
    return call(kernel, "next_column_sums", (stream, targets), (row,), (held, extra, row))[0]


def exchange(v, axes, flip):
    size = lax.axis_size(axes)
    return lax.ppermute(v, axes, [(i, i ^ flip) for i in range(size)])


def in_order(bit, v, other):
    first = bit == 0
    return jnp.concatenate([jnp.where(first, v, other), jnp.where(first, other, v)], axis=0)


def doubled(v, axes, flip, bit):
    return in_order(bit, v, exchange(v, axes, flip))


def norms(points):
    wide = points.astype(jnp.float32)
    return jnp.sum(wide * wide, axis=0)


def per_device(source, target, source_logw, target_logw, start_potential):
    z, y, xh, xl, core = (lax.axis_index(name) for name in names)
    width, span = source.shape[1], target.shape[1]

    sources = source[None]
    targets = jnp.concatenate([target, start_potential], axis=0)[None]
    other = exchange(sources, x, 1)
    sources = jnp.zeros((2, dim, width), sources.dtype)
    sources = lax.dynamic_update_slice(sources, source[None], (xl, 0, 0))
    sources = lax.dynamic_update_slice(sources, other, (1 - xl, 0, 0))
    targets = jnp.concatenate([targets, exchange(targets, x, 3)], axis=0)
    sources = doubled(sources, "z", 1, z % 2)
    targets = jnp.concatenate([targets, exchange(targets, "y", 3)], axis=0)
    sources = doubled(sources, "z", 3, z // 2)
    sources = doubled(sources, "core", 1, core)
    others = exchange(targets, "y", 1)

    lse, held, shift = first_row_sums(targets, sources)
    lse = next_row_sums(others, lse, held, shift)
    lse = log_add(lse, exchange(lse, "core", 1))
    lse = log_add(lse, exchange(lse, x, 1))
    count = lse.shape[1]
    logw = source_logw[None]
    received = exchange(jnp.concatenate([lse, logw], axis=1), "z", 1)
    lse = log_add(lse, received[:, :count])
    received = received[:, count:]
    logw = jnp.where(
        z % 2 == 0,
        jnp.concatenate([logw, received], axis=1),
        jnp.concatenate([received, logw], axis=1),
    )
    received = exchange(jnp.concatenate([lse, logw], axis=1), "z", 3)
    place = (z // 2).astype(jnp.int32).reshape(1)
    partial, stream = first_column_sums(others, sources, lse, received, logw, place)

    sent = exchange(partial, "y", 1)
    half = 2 * span
    partial = next_column_sums(stream, targets, 2, 2)
    partial = log_add(partial, sent[:, half:])
    more = exchange(partial, "y", 3)
    partial = next_column_sums(stream, targets, 1, 1)
    partial = log_add(log_add(partial, sent[:, span:half]), more[:, span:])
    last = exchange(partial, x, 3)
    partial = next_column_sums(stream, targets, 0, 1)
    partial = log_add(log_add(partial, sent[:, :span]), more[:, :span])
    partial = log_add(partial, last)[0]

    at = 2 * (z // 2) + z % 2
    lse = log_add(lse, received[:, : lse.shape[1]])
    mine = lax.dynamic_index_in_dim(lse.reshape(2, 4, 2, width), at, 1, False)
    mine = mine.transpose(1, 0, 2).reshape(4 * width)
    picked = sources[:, :dim, :].reshape(2, 4, 2, dim, width)
    picked = lax.dynamic_index_in_dim(picked, at, 1, False)
    row_sq = jnp.sum(jnp.square(picked.astype(jnp.float32)), axis=2)
    row_sq = row_sq.transpose(1, 0, 2).reshape(4 * width)
    row_lse = mine / log2e - row_sq / smoothing
    row_potential = smoothing * source_logw - smoothing * row_lse

    col_lse = partial / log2e - norms(target) / smoothing
    col_potential = smoothing * target_logw - smoothing * col_lse
    return (row_potential, col_potential)


def solution(mesh):
    devices = Mesh(mesh.devices.reshape(shape), names)
    rows = ("z", "y", "xh")
    columns_over = ("xl", "core", "z", "y", "xh")
    in_specs = (P(None, names), P(None, columns_over), P(rows), P(columns_over), P(None, columns_over))
    out_specs = (P(rows), P(columns_over))
    return jax.shard_map(
        per_device, mesh=devices, in_specs=in_specs, out_specs=out_specs, check_vma=False
    )
```

```python
import functools
import math

import jax
import jax.numpy as jnp
from jax import lax
from jax.experimental import pallas as pl
from jax.experimental.pallas import tpu as pltpu
from jax.sharding import Mesh
from jax.sharding import PartitionSpec as P

smoothing = 0.1
log2e = math.log2(math.e)
kappa = 2.0 * log2e / smoothing
scale = log2e / smoothing
dim = 64
headroom = 24.0
sample = 128
row_blocks = (1024, 1024)
column_blocks = (1024, 768)
largest = 3e38
smallest = 2.0**-90
shape = (4, 4, 2, 2, 2)
names = ("z", "y", "xh", "xl", "core")
x = ("xh", "xl")


def three_parts(v):
    hi = v.astype(jnp.bfloat16).astype(jnp.float32)
    mid = (v - hi).astype(jnp.bfloat16).astype(jnp.float32)
    return hi, mid, v - hi - mid


def rounded(v):
    return v.astype(jnp.bfloat16).astype(jnp.float32)


def log_add(a, b):
    top = jnp.maximum(a, b)
    return top + jnp.log2(1.0 + jnp.exp2(-jnp.abs(a - b)))


def streamed_features(points, bias):
    m = points.shape[1]
    hi, mid, lo = three_parts(bias)
    row = lax.broadcasted_iota(jnp.int32, (16, m), 0)
    extra = jnp.where(row == 0, hi, jnp.where(row == 1, mid, jnp.where(row == 2, lo, 0.0)))
    extra = jnp.where(row == 3, 1.0, extra).astype(jnp.bfloat16)
    block = jnp.concatenate([points, extra, jnp.zeros((48, m), jnp.bfloat16)], axis=0)
    return block.T


def fill_held(held_ref, start, points):
    cols = slice(start, start + points.shape[1])
    wide = points.astype(jnp.float32) * kappa
    hi = wide.astype(jnp.bfloat16)
    held_ref[:dim, cols] = hi
    held_ref[dim:, cols] = (wide - hi.astype(jnp.float32)).astype(jnp.bfloat16)


class LogSums:
    def __init__(self, stream_ref, held_ref, extra_ref, out_ref, shift_ref, blocks):
        self.stream_ref, self.held_ref, self.extra_ref = stream_ref, held_ref, extra_ref
        self.out_ref, self.shift_ref = out_ref, shift_ref
        self.chunk, self.tile = blocks
        self.m, self.n = stream_ref.shape[0], held_ref.shape[1]
        self.unroll = 2 if self.n // self.tile % 2 == 0 and self.n > 2000 else 1

    def scores(self, start, size, cols):
        u = self.stream_ref[pl.ds(start, size), :]
        held = self.held_ref[:, cols]
        zeros = jnp.zeros((dim, held.shape[1]), jnp.bfloat16)
        held = jnp.concatenate(
            [held[:dim], self.extra_ref[:, cols], zeros[:48], held[dim:], zeros], axis=0
        )
        return lax.dot_general(
            jnp.concatenate([u, u], axis=1),
            held,
            (((1,), (0,)), ((), ())),
            preferred_element_type=jnp.float32,
        )

    def set_extra(self, shift):
        row = lax.broadcasted_iota(jnp.int32, (16, self.n), 0)
        extra = jnp.where(row < 3, 1.0, jnp.where(row == 3, -shift, 0.0))
        self.extra_ref[...] = extra.astype(jnp.bfloat16)

    def tiles(self, step):
        def body(t, _):
            step(pl.ds(pl.multiple_of(t * self.tile, self.tile), self.tile))
            return 0

        lax.fori_loop(0, self.n // self.tile, body, 0, unroll=self.unroll)

    def estimate(self):
        self.set_extra(jnp.zeros((1, self.n), jnp.float32))
        top = jnp.max(self.scores(0, sample, slice(None)), axis=0, keepdims=True)
        self.shift_ref[...] = rounded(top + headroom)

    def sums(self):
        self.set_extra(self.shift_ref[...])

        def add_up(cols):
            acc = jnp.zeros((8, self.tile), jnp.float32)
            for c in range(self.m // self.chunk):
                e = jnp.exp2(self.scores(c * self.chunk, self.chunk, cols))
                acc = acc + jnp.sum(e.reshape(self.chunk // 8, 8, self.tile), axis=0)
            self.out_ref[:, cols] = jnp.sum(acc, axis=0, keepdims=True)

        self.tiles(add_up)
        return self.out_ref[...]

    def exact(self):
        self.set_extra(jnp.zeros((1, self.n), jnp.float32))

        def highest(cols):
            def step(c, acc):
                v = self.scores(pl.multiple_of(c * sample, sample), sample, cols)
                return jnp.maximum(acc, jnp.max(v, axis=0, keepdims=True))

            none = jnp.full((1, self.tile), -largest, jnp.float32)
            self.out_ref[:, cols] = lax.fori_loop(0, self.m // sample, step, none)

        self.tiles(highest)
        return self.out_ref[...]

    def run(self, prior=None):
        def attempt(state):
            total = self.sums()
            if prior is not None:
                total = total + jnp.exp2(prior - self.shift_ref[...])
            in_range = jnp.logical_and(jnp.max(total) < largest, jnp.min(total) > smallest)
            again = jnp.logical_not(in_range)
            self.out_ref[...] = self.shift_ref[...] + jnp.log2(total)

            @pl.when(again)
            def _():
                top = self.exact()
                self.shift_ref[...] = rounded(top if prior is None else jnp.maximum(top, prior))

            return state[0] + 1, again

        lax.while_loop(lambda s: jnp.logical_and(s[1], s[0] < 2), attempt, (0, True))


def fill_row_stream(t_ref, stream_ref, bias_ref):
    pieces, _, width = t_ref.shape
    for k in range(pieces):
        points = t_ref[k, :dim, :]
        lifted = t_ref[k, dim : dim + 1, :].astype(jnp.float32)
        wide = points.astype(jnp.float32)
        bias = scale * (lifted - jnp.sum(wide * wide, axis=0, keepdims=True))
        bias_ref[:, k * width : (k + 1) * width] = bias
        stream_ref[k * width : (k + 1) * width, :] = streamed_features(points, bias)


def first_row_kernel(t_ref, s_ref, out_ref, held_ref, shift_ref, bias_ref, stream_ref, extra_ref):
    fill_row_stream(t_ref, stream_ref, bias_ref)
    for k in range(s_ref.shape[0]):
        fill_held(held_ref, k * s_ref.shape[2], s_ref[k, :dim, :])
    sums = LogSums(stream_ref, held_ref, extra_ref, out_ref, shift_ref, row_blocks)
    sums.estimate()
    sums.run()


def next_row_kernel(
    t_ref, held_ref, old_ref, prior_ref, out_ref, bias_ref, stream_ref, extra_ref, shift_ref
):
    fill_row_stream(t_ref, stream_ref, bias_ref)
    shift_ref[...] = old_ref[...]
    LogSums(stream_ref, held_ref, extra_ref, out_ref, shift_ref, row_blocks).run(prior_ref[...])


def fill_column_stream(s_ref, lse_ref, received_ref, logw_ref, place_ref, stream_ref):
    pieces, _, width = s_ref.shape
    n = lse_ref.shape[1]
    half = logw_ref.shape[1]
    here, there = logw_ref[...], received_ref[:, n:]
    ordered = place_ref[0] == 0
    logw = (jnp.where(ordered, here, there), jnp.where(ordered, there, here))
    for k in range(pieces):
        core, hi, lo, xl = k // 8, k // 4 % 2, k // 2 % 2, k % 2
        at = lo * (half // 2) + (2 * xl + core) * width
        cols = slice(k * width, (k + 1) * width)
        lse = log_add(lse_ref[:, cols], received_ref[:, cols])
        bias = log2e * logw[hi][:, at : at + width] - lse
        stream_ref[cols, :] = streamed_features(s_ref[k], bias)


def columns(first, t_ref, bias_ref, out_ref, stream_ref, held_ref, extra_ref, shift_ref):
    width = t_ref.shape[2]
    start = first * width
    shift_ref[...] = rounded(-bias_ref[:, start : start + held_ref.shape[1]])
    for k in range(held_ref.shape[1] // width):
        fill_held(held_ref, k * width, t_ref[first + k, :dim, :])
    LogSums(stream_ref, held_ref, extra_ref, out_ref, shift_ref, column_blocks).run()


def first_column_kernel(*refs):
    ins, (t_ref, bias_ref, out_ref, stream_ref), scratch = refs[:-7], refs[-7:-3], refs[-3:]
    fill_column_stream(*ins, stream_ref)
    columns(0, t_ref, bias_ref, out_ref, stream_ref, *scratch)


def next_column_kernel(first, stream_ref, t_ref, bias_ref, out_ref, *scratch):
    columns(first, t_ref, bias_ref, out_ref, stream_ref, *scratch)


whole = pl.BlockSpec(memory_space=pltpu.VMEM)
scalar = pl.BlockSpec(memory_space=pltpu.SMEM)


def call(kernel, name, operands, outs, scratch, in_specs=None):
    return pl.pallas_call(
        kernel,
        in_specs=in_specs or [whole] * len(operands),
        out_specs=[whole] * len(outs),
        out_shape=[jax.ShapeDtypeStruct(*o) for o in outs],
        scratch_shapes=[pltpu.VMEM(*s) for s in scratch],
        compiler_params=pltpu.CompilerParams(vmem_limit_bytes=40 * 2**20),
        name=name,
    )(*operands)


def stream_of(points):
    return ((points, 128), jnp.bfloat16)


def arrays_of(n):
    row = ((1, n), jnp.float32)
    return row, ((2 * dim, n), jnp.bfloat16), ((16, n), jnp.bfloat16)


def points_of(targets):
    return targets.shape[0] * targets.shape[2]


def first_row_sums(targets, sources):
    row, held, extra = arrays_of(points_of(sources))
    outs = (row, held, row, arrays_of(points_of(targets))[0])
    scratch = (stream_of(points_of(targets)), extra)
    return call(first_row_kernel, "first_row_sums", (targets, sources), outs, scratch)


def next_row_sums(targets, prior, held, shift):
    row, _, extra = arrays_of(held.shape[1])
    outs = (row, arrays_of(points_of(targets))[0])
    scratch = (stream_of(points_of(targets)), extra, row)
    return call(next_row_kernel, "next_row_sums", (targets, held, shift, prior), outs, scratch)


def first_column_sums(targets, biases, sources, *more):
    row, held, extra = arrays_of(points_of(targets))
    operands = (sources, *more, targets, biases)
    specs = [scalar if v.dtype == jnp.int32 else whole for v in operands]
    outs = (row, stream_of(points_of(sources)))
    return call(first_column_kernel, "first_column_sums", operands, outs, (held, extra, row), specs)


def next_column_sums(stream, targets, biases, first, count):
    row, held, extra = arrays_of(count * targets.shape[2])
    kernel = functools.partial(next_column_kernel, first)
    operands = (stream, targets, biases)
    return call(kernel, "next_column_sums", operands, (row,), (held, extra, row))[0]


def exchange(v, axes, flip):
    size = lax.axis_size(axes)
    return lax.ppermute(v, axes, [(i, i ^ flip) for i in range(size)])


def in_order(bit, v, other):
    first = bit == 0
    return jnp.concatenate([jnp.where(first, v, other), jnp.where(first, other, v)], axis=0)


def doubled(v, axes, flip, bit):
    return in_order(bit, v, exchange(v, axes, flip))


def norms(points):
    wide = points.astype(jnp.float32)
    return jnp.sum(wide * wide, axis=0)


def per_device(source, target, source_logw, target_logw, start_potential):
    z, y, xh, xl, core = (lax.axis_index(name) for name in names)
    width, span = source.shape[1], target.shape[1]

    sources = source[None]
    targets = jnp.concatenate([target, start_potential], axis=0)[None]
    other = exchange(sources, x, 1)
    sources = jnp.zeros((2, dim, width), sources.dtype)
    sources = lax.dynamic_update_slice(sources, source[None], (xl, 0, 0))
    sources = lax.dynamic_update_slice(sources, other, (1 - xl, 0, 0))
    targets = jnp.concatenate([targets, exchange(targets, x, 3)], axis=0)
    sources = doubled(sources, "z", 1, z % 2)
    targets = jnp.concatenate([targets, exchange(targets, "y", 3)], axis=0)
    sources = doubled(sources, "z", 3, z // 2)
    sources = doubled(sources, "core", 1, core)
    others = exchange(targets, "y", 1)

    lse, held, shift, biases = first_row_sums(targets, sources)
    lse, other_biases = next_row_sums(others, lse, held, shift)
    lse = log_add(lse, exchange(lse, "core", 1))
    column_base = smoothing * target_logw
    lse, column_base = lax.optimization_barrier((lse, column_base))
    lse = log_add(lse, exchange(lse, x, 1))
    count = lse.shape[1]
    logw = source_logw[None]
    received = exchange(jnp.concatenate([lse, logw], axis=1), "z", 1)
    lse = log_add(lse, received[:, :count])
    received = received[:, count:]
    logw = jnp.where(
        z % 2 == 0,
        jnp.concatenate([logw, received], axis=1),
        jnp.concatenate([received, logw], axis=1),
    )
    received = exchange(jnp.concatenate([lse, logw], axis=1), "z", 3)
    place = (z // 2).astype(jnp.int32).reshape(1)
    partial, stream = first_column_sums(others, other_biases, sources, lse, received, logw, place)

    sent = exchange(partial, "y", 1)
    half = 2 * span
    partial = next_column_sums(stream, targets, biases, 2, 2)
    partial = log_add(partial, sent[:, half:])
    more = exchange(partial, "y", 3)
    partial = next_column_sums(stream, targets, biases, 1, 1)
    partial = log_add(log_add(partial, sent[:, span:half]), more[:, span:])
    last = exchange(partial, x, 3)
    partial = next_column_sums(stream, targets, biases, 0, 1)
    partial = log_add(log_add(partial, sent[:, :span]), more[:, :span])
    partial = log_add(partial, last)[0]

    at = 2 * (z // 2) + z % 2
    lse = log_add(lse, received[:, : lse.shape[1]])
    mine = lax.dynamic_index_in_dim(lse.reshape(2, 4, 2, width), at, 1, False)
    mine = mine.transpose(1, 0, 2).reshape(4 * width)
    picked = sources[:, :dim, :].reshape(2, 4, 2, dim, width)
    picked = lax.dynamic_index_in_dim(picked, at, 1, False)
    row_sq = jnp.sum(jnp.square(picked.astype(jnp.float32)), axis=2)
    row_sq = row_sq.transpose(1, 0, 2).reshape(4 * width)
    row_lse = mine / log2e - row_sq / smoothing
    row_potential = smoothing * source_logw - smoothing * row_lse

    col_lse = partial / log2e - norms(target) / smoothing
    col_potential = column_base - smoothing * col_lse
    return (row_potential, col_potential)


def solution(mesh):
    devices = Mesh(mesh.devices.reshape(shape), names)
    rows = ("z", "y", "xh")
    columns_over = ("xl", "core", "z", "y", "xh")
    in_specs = (P(None, names), P(None, columns_over), P(rows), P(columns_over), P(None, columns_over))
    out_specs = (P(rows), P(columns_over))
    return jax.shard_map(
        per_device, mesh=devices, in_specs=in_specs, out_specs=out_specs, check_vma=False
    )
```

```python
import functools
import math

import jax
import jax.numpy as jnp
from jax import lax
from jax.experimental import pallas as pl
from jax.experimental.pallas import tpu as pltpu
from jax.sharding import Mesh
from jax.sharding import PartitionSpec as P

smoothing = 0.1
log2e = math.log2(math.e)
kappa = 2.0 * log2e / smoothing
scale = log2e / smoothing
dim = 64
headroom = 48.0
sample = 32
redo_chunk = 256
row_blocks = (1024, 1024)
column_blocks = (1024, 768)
largest = 3e38
smallest = 2.0**-90
shape = (4, 4, 2, 2, 2)
names = ("z", "y", "xh", "xl", "core")
x = ("xh", "xl")
along_z = (0, 3, 1, 2)


def three_parts(v):
    hi = v.astype(jnp.bfloat16).astype(jnp.float32)
    mid = (v - hi).astype(jnp.bfloat16).astype(jnp.float32)
    return hi, mid, v - hi - mid


def rounded(v):
    return v.astype(jnp.bfloat16).astype(jnp.float32)


def log_add(a, b):
    top = jnp.maximum(a, b)
    return top + jnp.log2(1.0 + jnp.exp2(-jnp.abs(a - b)))


def streamed_features(points, bias):
    m = points.shape[1]
    hi, mid, lo = three_parts(bias)
    row = lax.broadcasted_iota(jnp.int32, (16, m), 0)
    extra = jnp.where(row == 0, hi, jnp.where(row == 1, mid, jnp.where(row == 2, lo, 0.0)))
    extra = jnp.where(row == 3, 1.0, extra).astype(jnp.bfloat16)
    block = jnp.concatenate([points, extra, jnp.zeros((48, m), jnp.bfloat16)], axis=0)
    return block.T


def fill_held(held_ref, start, points):
    cols = slice(start, start + points.shape[1])
    wide = points.astype(jnp.float32) * kappa
    hi = wide.astype(jnp.bfloat16)
    held_ref[:dim, cols] = hi
    held_ref[dim:, cols] = (wide - hi.astype(jnp.float32)).astype(jnp.bfloat16)


class LogSums:
    def __init__(self, stream_ref, held_ref, extra_ref, out_ref, shift_ref, blocks):
        self.stream_ref, self.held_ref, self.extra_ref = stream_ref, held_ref, extra_ref
        self.out_ref, self.shift_ref = out_ref, shift_ref
        self.chunk, self.tile = blocks
        self.m, self.n = stream_ref.shape[0], held_ref.shape[1]
        self.unroll = 2 if self.n // self.tile % 2 == 0 and self.n > 2000 else 1

    def scores(self, start, size, cols):
        u = self.stream_ref[pl.ds(start, size), :]
        held = self.held_ref[:, cols]
        zeros = jnp.zeros((dim, held.shape[1]), jnp.bfloat16)
        held = jnp.concatenate(
            [held[:dim], self.extra_ref[:, cols], zeros[:48], held[dim:], zeros], axis=0
        )
        return lax.dot_general(
            jnp.concatenate([u, u], axis=1),
            held,
            (((1,), (0,)), ((), ())),
            preferred_element_type=jnp.float32,
        )

    def set_extra(self, shift):
        row = lax.broadcasted_iota(jnp.int32, (16, self.n), 0)
        extra = jnp.where(row < 3, 1.0, jnp.where(row == 3, -shift, 0.0))
        self.extra_ref[...] = extra.astype(jnp.bfloat16)

    def tiles(self, step):
        def body(t, _):
            step(pl.ds(pl.multiple_of(t * self.tile, self.tile), self.tile))
            return 0

        lax.fori_loop(0, self.n // self.tile, body, 0, unroll=self.unroll)

    def estimate(self):
        self.set_extra(jnp.zeros((1, self.n), jnp.float32))
        top = jnp.max(self.scores(0, sample, slice(None)), axis=0, keepdims=True)
        self.shift_ref[...] = rounded(top + headroom)

    def sums(self):
        self.set_extra(self.shift_ref[...])

        def add_up(cols):
            acc = jnp.zeros((8, self.tile), jnp.float32)
            for c in range(self.m // self.chunk):
                e = jnp.exp2(self.scores(c * self.chunk, self.chunk, cols))
                acc = acc + jnp.sum(e.reshape(self.chunk // 8, 8, self.tile), axis=0)
            self.out_ref[:, cols] = jnp.sum(acc, axis=0, keepdims=True)

        self.tiles(add_up)
        return self.out_ref[...]

    def exact(self):
        self.set_extra(jnp.zeros((1, self.n), jnp.float32))

        def highest(cols):
            def step(c, acc):
                v = self.scores(pl.multiple_of(c * redo_chunk, redo_chunk), redo_chunk, cols)
                return jnp.maximum(acc, jnp.max(v, axis=0, keepdims=True))

            none = jnp.full((1, self.tile), -largest, jnp.float32)
            self.out_ref[:, cols] = lax.fori_loop(0, self.m // redo_chunk, step, none)

        self.tiles(highest)
        return self.out_ref[...]

    def run(self, prior=None):
        def attempt(state):
            total = self.sums()
            if prior is not None:
                total = total + jnp.exp2(prior - self.shift_ref[...])
            in_range = jnp.logical_and(jnp.max(total) < largest, jnp.min(total) > smallest)
            again = jnp.logical_not(in_range)
            self.out_ref[...] = self.shift_ref[...] + jnp.log2(total)

            @pl.when(again)
            def _():
                top = self.exact()
                self.shift_ref[...] = rounded(top if prior is None else jnp.maximum(top, prior))

            return state[0] + 1, again

        lax.while_loop(lambda s: jnp.logical_and(s[1], s[0] < 2), attempt, (0, True))


def fill_row_stream(t_ref, stream_ref, bias_ref):
    pieces, _, width = t_ref.shape
    for k in range(pieces):
        points = t_ref[k, :dim, :]
        lifted = t_ref[k, dim : dim + 1, :].astype(jnp.float32)
        wide = points.astype(jnp.float32)
        bias = scale * (lifted - jnp.sum(wide * wide, axis=0, keepdims=True))
        bias_ref[:, k * width : (k + 1) * width] = bias
        stream_ref[k * width : (k + 1) * width, :] = streamed_features(points, bias)


def first_row_kernel(t_ref, s_ref, out_ref, held_ref, shift_ref, bias_ref, stream_ref, extra_ref):
    fill_row_stream(t_ref, stream_ref, bias_ref)
    for k in range(s_ref.shape[0]):
        fill_held(held_ref, k * s_ref.shape[2], s_ref[k, :dim, :])
    sums = LogSums(stream_ref, held_ref, extra_ref, out_ref, shift_ref, row_blocks)
    sums.estimate()
    sums.run()


def next_row_kernel(
    t_ref, held_ref, old_ref, prior_ref, out_ref, bias_ref, stream_ref, extra_ref, shift_ref
):
    fill_row_stream(t_ref, stream_ref, bias_ref)
    shift_ref[...] = old_ref[...]
    LogSums(stream_ref, held_ref, extra_ref, out_ref, shift_ref, row_blocks).run(prior_ref[...])


def fill_column_stream(s_ref, lse_ref, received_ref, logw_ref, stream_ref):
    pieces, _, width = s_ref.shape
    per = pieces // len(along_z)
    for k in range(pieces):
        at = (along_z[k // per] * per + k % per) * width
        cols = slice(k * width, (k + 1) * width)
        lse = log_add(lse_ref[:, cols], received_ref[:, cols])
        bias = log2e * logw_ref[:, at : at + width] - lse
        stream_ref[cols, :] = streamed_features(s_ref[k], bias)


def columns(first, t_ref, bias_ref, out_ref, stream_ref, held_ref, extra_ref, shift_ref):
    width = t_ref.shape[2]
    start = first * width
    shift_ref[...] = rounded(-bias_ref[:, start : start + held_ref.shape[1]])
    for k in range(held_ref.shape[1] // width):
        fill_held(held_ref, k * width, t_ref[first + k, :dim, :])
    LogSums(stream_ref, held_ref, extra_ref, out_ref, shift_ref, column_blocks).run()


def first_column_kernel(*refs):
    ins, (t_ref, bias_ref, out_ref, stream_ref), scratch = refs[:-7], refs[-7:-3], refs[-3:]
    fill_column_stream(*ins, stream_ref)
    columns(0, t_ref, bias_ref, out_ref, stream_ref, *scratch)


def next_column_kernel(first, stream_ref, t_ref, bias_ref, out_ref, *scratch):
    columns(first, t_ref, bias_ref, out_ref, stream_ref, *scratch)


whole = pl.BlockSpec(memory_space=pltpu.VMEM)


def call(kernel, name, operands, outs, scratch):
    return pl.pallas_call(
        kernel,
        in_specs=[whole] * len(operands),
        out_specs=[whole] * len(outs),
        out_shape=[jax.ShapeDtypeStruct(*o) for o in outs],
        scratch_shapes=[pltpu.VMEM(*s) for s in scratch],
        compiler_params=pltpu.CompilerParams(vmem_limit_bytes=40 * 2**20),
        name=name,
    )(*operands)


def stream_of(points):
    return ((points, 128), jnp.bfloat16)


def arrays_of(n):
    row = ((1, n), jnp.float32)
    return row, ((2 * dim, n), jnp.bfloat16), ((16, n), jnp.bfloat16)


def points_of(targets):
    return targets.shape[0] * targets.shape[2]


def first_row_sums(targets, sources):
    row, held, extra = arrays_of(points_of(sources))
    outs = (row, held, row, arrays_of(points_of(targets))[0])
    scratch = (stream_of(points_of(targets)), extra)
    return call(first_row_kernel, "first_row_sums", (targets, sources), outs, scratch)


def next_row_sums(targets, prior, held, shift):
    row, _, extra = arrays_of(held.shape[1])
    outs = (row, arrays_of(points_of(targets))[0])
    scratch = (stream_of(points_of(targets)), extra, row)
    return call(next_row_kernel, "next_row_sums", (targets, held, shift, prior), outs, scratch)


def first_column_sums(targets, biases, sources, *more):
    row, held, extra = arrays_of(points_of(targets))
    operands = (sources, *more, targets, biases)
    outs = (row, stream_of(points_of(sources)))
    return call(first_column_kernel, "first_column_sums", operands, outs, (held, extra, row))


def next_column_sums(stream, targets, biases, first, count):
    row, held, extra = arrays_of(count * targets.shape[2])
    kernel = functools.partial(next_column_kernel, first)
    operands = (stream, targets, biases)
    return call(kernel, "next_column_sums", operands, (row,), (held, extra, row))[0]


def exchange(v, axes, flip):
    size = lax.axis_size(axes)
    return lax.ppermute(v, axes, [(i, i ^ flip) for i in range(size)])


def in_order(bit, v, other):
    first = bit == 0
    return jnp.concatenate([jnp.where(first, v, other), jnp.where(first, other, v)], axis=0)


def doubled(v, axes, flip, bit):
    return in_order(bit, v, exchange(v, axes, flip))


def norms(points):
    wide = points.astype(jnp.float32)
    return jnp.sum(wide * wide, axis=0)


def per_device(source, target, source_logw, target_logw, start_potential):
    z, y, xh, xl, core = (lax.axis_index(name) for name in names)
    width, span = source.shape[1], target.shape[1]

    sources = source[None]
    targets = jnp.concatenate([target, start_potential], axis=0)[None]
    other = exchange(sources, "core", 1)
    sources = jnp.zeros((2, dim, width), sources.dtype)
    sources = lax.dynamic_update_slice(sources, source[None], (core, 0, 0))
    sources = lax.dynamic_update_slice(sources, other, (1 - core, 0, 0))
    sources = doubled(sources, x, 1, xl)
    targets = jnp.concatenate([targets, exchange(targets, x, 3)], axis=0)
    sources = doubled(sources, "z", 3, z // 2)
    targets = jnp.concatenate([targets, exchange(targets, "y", 3)], axis=0)
    sources = doubled(sources, "z", 1, (z ^ z // 2) % 2)
    others = exchange(targets, "y", 1)

    lse, held, shift, biases = first_row_sums(targets, sources)
    lse, other_biases = next_row_sums(others, lse, held, shift)
    column_base = smoothing * target_logw
    lse, column_base = lax.optimization_barrier((lse, column_base))
    lse = log_add(lse, exchange(lse, "core", 1))
    count = lse.shape[1]
    logw = source_logw[None]
    for flip, bit in ((1, z % 2), (3, z // 2)):
        received = exchange(jnp.concatenate([lse, logw], axis=1), "z", flip)
        lse = log_add(lse, received[:, :count])
        received = received[:, count:]
        logw = jnp.where(
            bit == 0,
            jnp.concatenate([logw, received], axis=1),
            jnp.concatenate([received, logw], axis=1),
        )
    received = exchange(lse, x, 1)
    partial, stream = first_column_sums(others, other_biases, sources, lse, received, logw)
    sent = exchange(partial, "y", 1)
    half = 2 * span
    partial = next_column_sums(stream, targets, biases, 2, 2)
    partial = log_add(partial, sent[:, half:])
    more = exchange(partial, "y", 3)
    partial = next_column_sums(stream, targets, biases, 1, 1)
    partial = log_add(log_add(partial, sent[:, span:half]), more[:, span:])
    last = exchange(partial, x, 3)
    partial = next_column_sums(stream, targets, biases, 0, 1)
    partial = log_add(log_add(partial, sent[:, :span]), more[:, :span])
    partial = log_add(partial, last)[0]

    at = 2 * ((z ^ z // 2) % 2) + z // 2
    lse = log_add(lse, received)
    mine = lax.dynamic_index_in_dim(lse.reshape(4, 4 * width), at, 0, False)
    picked = lax.dynamic_index_in_dim(sources.reshape(4, 4, dim, width), at, 0, False)
    row_sq = jnp.sum(jnp.square(picked.astype(jnp.float32)), axis=1).reshape(4 * width)
    row_lse = mine / log2e - row_sq / smoothing
    row_potential = smoothing * source_logw - smoothing * row_lse

    col_lse = partial / log2e - norms(target) / smoothing
    col_potential = column_base - smoothing * col_lse
    return (row_potential, col_potential)


def solution(mesh):
    devices = Mesh(mesh.devices.reshape(shape), names)
    rows = ("z", "y", "xh")
    columns_over = ("xl", "core", "z", "y", "xh")
    in_specs = (P(None, names), P(None, columns_over), P(rows), P(columns_over), P(None, columns_over))
    out_specs = (P(rows), P(columns_over))
    return jax.shard_map(
        per_device, mesh=devices, in_specs=in_specs, out_specs=out_specs, check_vma=False
    )
```

```python
import functools
import math

import jax
import jax.numpy as jnp
from jax import lax
from jax.experimental import pallas as pl
from jax.experimental.pallas import tpu as pltpu
from jax.sharding import Mesh
from jax.sharding import PartitionSpec as P

smoothing = 0.1
log2e = math.log2(math.e)
kappa = 2.0 * log2e / smoothing
scale = log2e / smoothing
dim = 64
headroom = 48.0
sample = 32
redo_chunk = 256
row_blocks = (1024, 1024)
column_blocks = (1024, 768)
largest = 3e38
smallest = 2.0**-90
shape = (4, 4, 2, 2, 2)
names = ("z", "y", "xh", "xl", "core")
x = ("xh", "xl")
along_z = (0, 1, 2, 3)


def three_parts(v):
    hi = v.astype(jnp.bfloat16).astype(jnp.float32)
    mid = (v - hi).astype(jnp.bfloat16).astype(jnp.float32)
    return hi, mid, v - hi - mid


def rounded(v):
    return v.astype(jnp.bfloat16).astype(jnp.float32)


def log_add(a, b):
    top = jnp.maximum(a, b)
    return top + jnp.log2(1.0 + jnp.exp2(-jnp.abs(a - b)))


def streamed_features(points, bias):
    m = points.shape[1]
    hi, mid, lo = three_parts(bias)
    row = lax.broadcasted_iota(jnp.int32, (16, m), 0)
    extra = jnp.where(row == 0, hi, jnp.where(row == 1, mid, jnp.where(row == 2, lo, 0.0)))
    extra = jnp.where(row == 3, 1.0, extra).astype(jnp.bfloat16)
    block = jnp.concatenate([points, extra, jnp.zeros((48, m), jnp.bfloat16)], axis=0)
    return block.T


def fill_held(held_ref, start, points):
    cols = slice(start, start + points.shape[1])
    wide = points.astype(jnp.float32) * kappa
    hi = wide.astype(jnp.bfloat16)
    held_ref[:dim, cols] = hi
    held_ref[dim:, cols] = (wide - hi.astype(jnp.float32)).astype(jnp.bfloat16)


class LogSums:
    def __init__(self, stream_ref, held_ref, extra_ref, out_ref, shift_ref, blocks):
        self.stream_ref, self.held_ref, self.extra_ref = stream_ref, held_ref, extra_ref
        self.out_ref, self.shift_ref = out_ref, shift_ref
        self.chunk, self.tile = blocks
        self.m, self.n = stream_ref.shape[0], held_ref.shape[1]
        self.unroll = 2 if self.n // self.tile % 2 == 0 and self.n > 2000 else 1

    def scores(self, start, size, cols):
        u = self.stream_ref[pl.ds(start, size), :]
        held = self.held_ref[:, cols]
        zeros = jnp.zeros((dim, held.shape[1]), jnp.bfloat16)
        held = jnp.concatenate(
            [held[:dim], self.extra_ref[:, cols], zeros[:48], held[dim:], zeros], axis=0
        )
        return lax.dot_general(
            jnp.concatenate([u, u], axis=1),
            held,
            (((1,), (0,)), ((), ())),
            preferred_element_type=jnp.float32,
        )

    def set_extra(self, shift):
        row = lax.broadcasted_iota(jnp.int32, (16, self.n), 0)
        extra = jnp.where(row < 3, 1.0, jnp.where(row == 3, -shift, 0.0))
        self.extra_ref[...] = extra.astype(jnp.bfloat16)

    def tiles(self, step):
        def body(t, _):
            step(pl.ds(pl.multiple_of(t * self.tile, self.tile), self.tile))
            return 0

        lax.fori_loop(0, self.n // self.tile, body, 0, unroll=self.unroll)

    def estimate(self):
        self.set_extra(jnp.zeros((1, self.n), jnp.float32))
        top = jnp.max(self.scores(0, sample, slice(None)), axis=0, keepdims=True)
        self.shift_ref[...] = rounded(top + headroom)

    def sums(self):
        self.set_extra(self.shift_ref[...])

        def add_up(cols):
            acc = jnp.zeros((8, self.tile), jnp.float32)
            for c in range(self.m // self.chunk):
                e = jnp.exp2(self.scores(c * self.chunk, self.chunk, cols))
                acc = acc + jnp.sum(e.reshape(self.chunk // 8, 8, self.tile), axis=0)
            self.out_ref[:, cols] = jnp.sum(acc, axis=0, keepdims=True)

        self.tiles(add_up)
        return self.out_ref[...]

    def exact(self):
        self.set_extra(jnp.zeros((1, self.n), jnp.float32))

        def highest(cols):
            def step(c, acc):
                v = self.scores(pl.multiple_of(c * redo_chunk, redo_chunk), redo_chunk, cols)
                return jnp.maximum(acc, jnp.max(v, axis=0, keepdims=True))

            none = jnp.full((1, self.tile), -largest, jnp.float32)
            self.out_ref[:, cols] = lax.fori_loop(0, self.m // redo_chunk, step, none)

        self.tiles(highest)
        return self.out_ref[...]

    def run(self, prior=None):
        def attempt(state):
            total = self.sums()
            if prior is not None:
                total = total + jnp.exp2(prior - self.shift_ref[...])
            in_range = jnp.logical_and(jnp.max(total) < largest, jnp.min(total) > smallest)
            again = jnp.logical_not(in_range)
            self.out_ref[...] = self.shift_ref[...] + jnp.log2(total)

            @pl.when(again)
            def _():
                top = self.exact()
                self.shift_ref[...] = rounded(top if prior is None else jnp.maximum(top, prior))

            return state[0] + 1, again

        lax.while_loop(lambda s: jnp.logical_and(s[1], s[0] < 2), attempt, (0, True))


def fill_row_stream(t_ref, stream_ref, bias_ref):
    pieces, _, width = t_ref.shape
    for k in range(pieces):
        points = t_ref[k, :dim, :]
        lifted = t_ref[k, dim : dim + 1, :].astype(jnp.float32)
        wide = points.astype(jnp.float32)
        bias = scale * (lifted - jnp.sum(wide * wide, axis=0, keepdims=True))
        bias_ref[:, k * width : (k + 1) * width] = bias
        stream_ref[k * width : (k + 1) * width, :] = streamed_features(points, bias)


def first_row_kernel(t_ref, s_ref, out_ref, held_ref, shift_ref, bias_ref, stream_ref, extra_ref):
    fill_row_stream(t_ref, stream_ref, bias_ref)
    for k in range(s_ref.shape[0]):
        fill_held(held_ref, k * s_ref.shape[2], s_ref[k, :dim, :])
    sums = LogSums(stream_ref, held_ref, extra_ref, out_ref, shift_ref, row_blocks)
    sums.estimate()
    sums.run()


def next_row_kernel(
    t_ref, held_ref, old_ref, prior_ref, out_ref, bias_ref, stream_ref, extra_ref, shift_ref
):
    fill_row_stream(t_ref, stream_ref, bias_ref)
    shift_ref[...] = old_ref[...]
    LogSums(stream_ref, held_ref, extra_ref, out_ref, shift_ref, row_blocks).run(prior_ref[...])


def fill_column_stream(s_ref, lse_ref, received_ref, logw_ref, stream_ref):
    pieces, _, width = s_ref.shape
    per = pieces // len(along_z)
    for k in range(pieces):
        at = (along_z[k // per] * per + k % per) * width
        cols = slice(k * width, (k + 1) * width)
        lse = log_add(lse_ref[:, cols], received_ref[:, cols])
        bias = log2e * logw_ref[:, at : at + width] - lse
        stream_ref[cols, :] = streamed_features(s_ref[k], bias)


def columns(first, t_ref, bias_ref, out_ref, stream_ref, held_ref, extra_ref, shift_ref):
    width = t_ref.shape[2]
    start = first * width
    shift_ref[...] = rounded(-bias_ref[:, start : start + held_ref.shape[1]])
    for k in range(held_ref.shape[1] // width):
        fill_held(held_ref, k * width, t_ref[first + k, :dim, :])
    LogSums(stream_ref, held_ref, extra_ref, out_ref, shift_ref, column_blocks).run()


def first_column_kernel(*refs):
    ins, (t_ref, bias_ref, out_ref, stream_ref), scratch = refs[:-7], refs[-7:-3], refs[-3:]
    fill_column_stream(*ins, stream_ref)
    columns(0, t_ref, bias_ref, out_ref, stream_ref, *scratch)


def next_column_kernel(first, stream_ref, t_ref, bias_ref, out_ref, *scratch):
    columns(first, t_ref, bias_ref, out_ref, stream_ref, *scratch)


whole = pl.BlockSpec(memory_space=pltpu.VMEM)


def call(kernel, name, operands, outs, scratch):
    return pl.pallas_call(
        kernel,
        in_specs=[whole] * len(operands),
        out_specs=[whole] * len(outs),
        out_shape=[jax.ShapeDtypeStruct(*o) for o in outs],
        scratch_shapes=[pltpu.VMEM(*s) for s in scratch],
        compiler_params=pltpu.CompilerParams(vmem_limit_bytes=40 * 2**20),
        name=name,
    )(*operands)


def stream_of(points):
    return ((points, 128), jnp.bfloat16)


def arrays_of(n):
    row = ((1, n), jnp.float32)
    return row, ((2 * dim, n), jnp.bfloat16), ((16, n), jnp.bfloat16)


def points_of(targets):
    return targets.shape[0] * targets.shape[2]


def first_row_sums(targets, sources):
    row, held, extra = arrays_of(points_of(sources))
    outs = (row, held, row, arrays_of(points_of(targets))[0])
    scratch = (stream_of(points_of(targets)), extra)
    return call(first_row_kernel, "first_row_sums", (targets, sources), outs, scratch)


def next_row_sums(targets, prior, held, shift):
    row, _, extra = arrays_of(held.shape[1])
    outs = (row, arrays_of(points_of(targets))[0])
    scratch = (stream_of(points_of(targets)), extra, row)
    return call(next_row_kernel, "next_row_sums", (targets, held, shift, prior), outs, scratch)


def first_column_sums(targets, biases, sources, *more):
    row, held, extra = arrays_of(points_of(targets))
    operands = (sources, *more, targets, biases)
    outs = (row, stream_of(points_of(sources)))
    return call(first_column_kernel, "first_column_sums", operands, outs, (held, extra, row))


def next_column_sums(stream, targets, biases, first, count):
    row, held, extra = arrays_of(count * targets.shape[2])
    kernel = functools.partial(next_column_kernel, first)
    operands = (stream, targets, biases)
    return call(kernel, "next_column_sums", operands, (row,), (held, extra, row))[0]


def exchange(v, axes, flip):
    size = lax.axis_size(axes)
    return lax.ppermute(v, axes, [(i, i ^ flip) for i in range(size)])


def in_order(bit, v, other):
    first = bit == 0
    return jnp.concatenate([jnp.where(first, v, other), jnp.where(first, other, v)], axis=0)


def doubled(v, axes, flip, bit):
    return in_order(bit, v, exchange(v, axes, flip))


def all_along_z(v, z, axis):
    near, wrap, far = (exchange(v, "z", flip) for flip in (1, 3, 2))
    even, low = z % 2 == 0, z < 2
    own = jnp.concatenate([jnp.where(even, v, near), jnp.where(even, near, v)], axis=axis)
    other = jnp.concatenate([jnp.where(even, far, wrap), jnp.where(even, wrap, far)], axis=axis)
    return jnp.concatenate([jnp.where(low, own, other), jnp.where(low, other, own)], axis=axis)


def norms(points):
    wide = points.astype(jnp.float32)
    return jnp.sum(wide * wide, axis=0)


def per_device(source, target, source_logw, target_logw, start_potential):
    z, y, xh, xl, core = (lax.axis_index(name) for name in names)
    width, span = source.shape[1], target.shape[1]

    sources = source[None]
    targets = jnp.concatenate([target, start_potential], axis=0)[None]
    other = exchange(sources, "core", 1)
    sources = jnp.zeros((2, dim, width), sources.dtype)
    sources = lax.dynamic_update_slice(sources, source[None], (core, 0, 0))
    sources = lax.dynamic_update_slice(sources, other, (1 - core, 0, 0))
    sources = doubled(sources, x, 1, xl)
    direct = [exchange(targets, axes, flip) for axes, flip in ((x, 3), ("y", 3), (("y", *x), 15))]
    targets = jnp.concatenate([targets, *direct], axis=0)
    sources = all_along_z(sources, z, 0)
    others = exchange(targets, "y", 1)

    lse, held, shift, biases = first_row_sums(targets, sources)
    lse, other_biases = next_row_sums(others, lse, held, shift)
    column_base = smoothing * target_logw
    lse, column_base = lax.optimization_barrier((lse, column_base))
    lse = log_add(lse, exchange(lse, "core", 1))
    count = lse.shape[1]
    logw = source_logw[None]
    received = [exchange(jnp.concatenate([lse, logw], axis=1), "z", flip) for flip in (1, 3, 2)]
    parts = [v[:, :count] for v in received]
    lse = log_add(log_add(lse, parts[0]), log_add(parts[1], parts[2]))
    near, wrap, far = (v[:, count:] for v in received)
    even, low = z % 2 == 0, z < 2
    own = jnp.concatenate([jnp.where(even, logw, near), jnp.where(even, near, logw)], axis=1)
    other = jnp.concatenate([jnp.where(even, far, wrap), jnp.where(even, wrap, far)], axis=1)
    logw = jnp.where(
        low, jnp.concatenate([own, other], axis=1), jnp.concatenate([other, own], axis=1)
    )
    received = exchange(lse, x, 1)
    partial, stream = first_column_sums(others, other_biases, sources, lse, received, logw)
    sent = exchange(partial, "y", 1)
    half = 2 * span
    partial = next_column_sums(stream, targets, biases, 2, 2)
    partial = log_add(partial, sent[:, half:])
    more = exchange(partial, "y", 3)
    partial = next_column_sums(stream, targets, biases, 1, 1)
    partial = log_add(log_add(partial, sent[:, span:half]), more[:, span:])

    at = z
    lse = log_add(lse, received)
    mine = lax.dynamic_index_in_dim(lse.reshape(4, 4 * width), at, 0, False)
    picked = lax.dynamic_index_in_dim(sources.reshape(4, 4, dim, width), at, 0, False)
    row_sq = jnp.sum(jnp.square(picked.astype(jnp.float32)), axis=1).reshape(4 * width)
    row_lse = mine / log2e - row_sq / smoothing
    row_potential = smoothing * source_logw - smoothing * row_lse
    partial, row_potential = lax.optimization_barrier((partial, row_potential))
    last = exchange(partial, x, 3)
    partial = next_column_sums(stream, targets, biases, 0, 1)
    partial = log_add(log_add(partial, sent[:, :span]), more[:, :span])
    partial = log_add(partial, last)[0]

    col_lse = partial / log2e - norms(target) / smoothing
    col_potential = column_base - smoothing * col_lse
    return (row_potential, col_potential)


def solution(mesh):
    devices = Mesh(mesh.devices.reshape(shape), names)
    rows = ("z", "y", "xh")
    columns_over = ("xl", "core", "z", "y", "xh")
    in_specs = (P(None, names), P(None, columns_over), P(rows), P(columns_over), P(None, columns_over))
    out_specs = (P(rows), P(columns_over))
    return jax.shard_map(
        per_device, mesh=devices, in_specs=in_specs, out_specs=out_specs, check_vma=False
    )
```

```python
import functools
import math

import jax
import jax.numpy as jnp
from jax import lax
from jax.experimental import pallas as pl
from jax.experimental.pallas import tpu as pltpu
from jax.sharding import Mesh
from jax.sharding import PartitionSpec as P

smoothing = 0.1
log2e = math.log2(math.e)
kappa = 2.0 * log2e / smoothing
scale = log2e / smoothing
dim = 64
headroom = 48.0
sample = 32
redo_chunk = 256
row_blocks = (1024, 1024)
column_blocks = (1024, 768)
largest = 3e38
smallest = 2.0**-90
shape = (4, 4, 2, 2, 2)
names = ("z", "y", "xh", "xl", "core")
x = ("xh", "xl")
along_z = (0, 1, 2, 3)


def three_parts(v):
    hi = v.astype(jnp.bfloat16).astype(jnp.float32)
    mid = (v - hi).astype(jnp.bfloat16).astype(jnp.float32)
    return hi, mid, v - hi - mid


def rounded(v):
    return v.astype(jnp.bfloat16).astype(jnp.float32)


def log_add(a, b):
    top = jnp.maximum(a, b)
    return top + jnp.log2(1.0 + jnp.exp2(-jnp.abs(a - b)))


def streamed_features(points, bias):
    m = points.shape[1]
    hi, mid, lo = three_parts(bias)
    row = lax.broadcasted_iota(jnp.int32, (16, m), 0)
    extra = jnp.where(row == 0, hi, jnp.where(row == 1, mid, jnp.where(row == 2, lo, 0.0)))
    extra = jnp.where(row == 3, 1.0, extra).astype(jnp.bfloat16)
    block = jnp.concatenate([points, extra, jnp.zeros((48, m), jnp.bfloat16)], axis=0)
    return block.T


def fill_held(held_ref, start, points):
    cols = slice(start, start + points.shape[1])
    wide = points.astype(jnp.float32) * kappa
    hi = wide.astype(jnp.bfloat16)
    held_ref[:dim, cols] = hi
    held_ref[dim:, cols] = (wide - hi.astype(jnp.float32)).astype(jnp.bfloat16)


class LogSums:
    def __init__(self, stream_ref, held_ref, extra_ref, out_ref, shift_ref, blocks):
        self.stream_ref, self.held_ref, self.extra_ref = stream_ref, held_ref, extra_ref
        self.out_ref, self.shift_ref = out_ref, shift_ref
        self.chunk, self.tile = blocks
        self.m, self.n = stream_ref.shape[0], held_ref.shape[1]
        self.unroll = 2 if self.n // self.tile % 2 == 0 and self.n > 2000 else 1

    def scores(self, start, size, cols):
        u = self.stream_ref[pl.ds(start, size), :]
        held = self.held_ref[:, cols]
        zeros = jnp.zeros((dim, held.shape[1]), jnp.bfloat16)
        held = jnp.concatenate(
            [held[:dim], self.extra_ref[:, cols], zeros[:48], held[dim:], zeros], axis=0
        )
        return lax.dot_general(
            jnp.concatenate([u, u], axis=1),
            held,
            (((1,), (0,)), ((), ())),
            preferred_element_type=jnp.float32,
        )

    def set_extra(self, shift):
        row = lax.broadcasted_iota(jnp.int32, (16, self.n), 0)
        extra = jnp.where(row < 3, 1.0, jnp.where(row == 3, -shift, 0.0))
        self.extra_ref[...] = extra.astype(jnp.bfloat16)

    def tiles(self, step):
        def body(t, _):
            step(pl.ds(pl.multiple_of(t * self.tile, self.tile), self.tile))
            return 0

        lax.fori_loop(0, self.n // self.tile, body, 0, unroll=self.unroll)

    def estimate(self):
        self.set_extra(jnp.zeros((1, self.n), jnp.float32))
        top = jnp.max(self.scores(0, sample, slice(None)), axis=0, keepdims=True)
        self.shift_ref[...] = rounded(top + headroom)

    def sums(self):
        self.set_extra(self.shift_ref[...])

        def add_up(cols):
            acc = jnp.zeros((8, self.tile), jnp.float32)
            for c in range(self.m // self.chunk):
                e = jnp.exp2(self.scores(c * self.chunk, self.chunk, cols))
                acc = acc + jnp.sum(e.reshape(self.chunk // 8, 8, self.tile), axis=0)
            self.out_ref[:, cols] = jnp.sum(acc, axis=0, keepdims=True)

        self.tiles(add_up)
        return self.out_ref[...]

    def exact(self):
        self.set_extra(jnp.zeros((1, self.n), jnp.float32))

        def highest(cols):
            def step(c, acc):
                v = self.scores(pl.multiple_of(c * redo_chunk, redo_chunk), redo_chunk, cols)
                return jnp.maximum(acc, jnp.max(v, axis=0, keepdims=True))

            none = jnp.full((1, self.tile), -largest, jnp.float32)
            self.out_ref[:, cols] = lax.fori_loop(0, self.m // redo_chunk, step, none)

        self.tiles(highest)
        return self.out_ref[...]

    def run(self, prior=None):
        def attempt(state):
            total = self.sums()
            if prior is not None:
                total = total + jnp.exp2(prior - self.shift_ref[...])
            in_range = jnp.logical_and(jnp.max(total) < largest, jnp.min(total) > smallest)
            again = jnp.logical_not(in_range)
            self.out_ref[...] = self.shift_ref[...] + jnp.log2(total)

            @pl.when(again)
            def _():
                top = self.exact()
                self.shift_ref[...] = rounded(top if prior is None else jnp.maximum(top, prior))

            return state[0] + 1, again

        lax.while_loop(lambda s: jnp.logical_and(s[1], s[0] < 2), attempt, (0, True))


def fill_row_stream(t_ref, stream_ref, bias_ref):
    pieces, _, width = t_ref.shape
    for k in range(pieces):
        points = t_ref[k, :dim, :]
        lifted = t_ref[k, dim : dim + 1, :].astype(jnp.float32)
        wide = points.astype(jnp.float32)
        bias = scale * (lifted - jnp.sum(wide * wide, axis=0, keepdims=True))
        bias_ref[:, k * width : (k + 1) * width] = bias
        stream_ref[k * width : (k + 1) * width, :] = streamed_features(points, bias)


def first_row_kernel(t_ref, s_ref, out_ref, held_ref, shift_ref, bias_ref, stream_ref, extra_ref):
    fill_row_stream(t_ref, stream_ref, bias_ref)
    for k in range(s_ref.shape[0]):
        fill_held(held_ref, k * s_ref.shape[2], s_ref[k, :dim, :])
    sums = LogSums(stream_ref, held_ref, extra_ref, out_ref, shift_ref, row_blocks)
    sums.estimate()
    sums.run()


def next_row_kernel(
    t_ref, held_ref, old_ref, prior_ref, out_ref, bias_ref, stream_ref, extra_ref, shift_ref
):
    fill_row_stream(t_ref, stream_ref, bias_ref)
    shift_ref[...] = old_ref[...]
    LogSums(stream_ref, held_ref, extra_ref, out_ref, shift_ref, row_blocks).run(prior_ref[...])


def fill_column_stream(s_ref, lse_ref, near_ref, far_ref, logw_ref, stream_ref):
    pieces, _, width = s_ref.shape
    per = pieces // len(along_z)
    for k in range(pieces):
        at = (along_z[k // per] * per + k % per) * width
        cols = slice(k * width, (k + 1) * width)
        lse = log_add(lse_ref[:, cols], log_add(near_ref[:, cols], far_ref[:, cols]))
        bias = log2e * logw_ref[:, at : at + width] - lse
        stream_ref[cols, :] = streamed_features(s_ref[k], bias)


def columns(first, t_ref, bias_ref, out_ref, stream_ref, held_ref, extra_ref, shift_ref):
    width = t_ref.shape[2]
    start = first * width
    shift_ref[...] = rounded(-bias_ref[:, start : start + held_ref.shape[1]])
    for k in range(held_ref.shape[1] // width):
        fill_held(held_ref, k * width, t_ref[first + k, :dim, :])
    LogSums(stream_ref, held_ref, extra_ref, out_ref, shift_ref, column_blocks).run()


def first_column_kernel(*refs):
    ins, (t_ref, bias_ref, out_ref, stream_ref), scratch = refs[:-7], refs[-7:-3], refs[-3:]
    fill_column_stream(*ins, stream_ref)
    columns(0, t_ref, bias_ref, out_ref, stream_ref, *scratch)


def next_column_kernel(first, stream_ref, t_ref, bias_ref, out_ref, *scratch):
    columns(first, t_ref, bias_ref, out_ref, stream_ref, *scratch)


whole = pl.BlockSpec(memory_space=pltpu.VMEM)


def call(kernel, name, operands, outs, scratch):
    return pl.pallas_call(
        kernel,
        in_specs=[whole] * len(operands),
        out_specs=[whole] * len(outs),
        out_shape=[jax.ShapeDtypeStruct(*o) for o in outs],
        scratch_shapes=[pltpu.VMEM(*s) for s in scratch],
        compiler_params=pltpu.CompilerParams(vmem_limit_bytes=40 * 2**20),
        name=name,
    )(*operands)


def stream_of(points):
    return ((points, 128), jnp.bfloat16)


def arrays_of(n):
    row = ((1, n), jnp.float32)
    return row, ((2 * dim, n), jnp.bfloat16), ((16, n), jnp.bfloat16)


def points_of(targets):
    return targets.shape[0] * targets.shape[2]


def first_row_sums(targets, sources):
    row, held, extra = arrays_of(points_of(sources))
    outs = (row, held, row, arrays_of(points_of(targets))[0])
    scratch = (stream_of(points_of(targets)), extra)
    return call(first_row_kernel, "first_row_sums", (targets, sources), outs, scratch)


def next_row_sums(targets, prior, held, shift):
    row, _, extra = arrays_of(held.shape[1])
    outs = (row, arrays_of(points_of(targets))[0])
    scratch = (stream_of(points_of(targets)), extra, row)
    return call(next_row_kernel, "next_row_sums", (targets, held, shift, prior), outs, scratch)


def first_column_sums(targets, biases, sources, *more):
    row, held, extra = arrays_of(points_of(targets))
    operands = (sources, *more, targets, biases)
    outs = (row, stream_of(points_of(sources)))
    return call(first_column_kernel, "first_column_sums", operands, outs, (held, extra, row))


def next_column_sums(stream, targets, biases, first, count):
    row, held, extra = arrays_of(count * targets.shape[2])
    kernel = functools.partial(next_column_kernel, first)
    operands = (stream, targets, biases)
    return call(kernel, "next_column_sums", operands, (row,), (held, extra, row))[0]


def exchange(v, axes, flip):
    size = lax.axis_size(axes)
    return lax.ppermute(v, axes, [(i, i ^ flip) for i in range(size)])


def in_order(bit, v, other):
    first = bit == 0
    return jnp.concatenate([jnp.where(first, v, other), jnp.where(first, other, v)], axis=0)


def doubled(v, axes, flip, bit):
    return in_order(bit, v, exchange(v, axes, flip))


def all_along_z(v, z, axis):
    far, wrap, near = (exchange(v, "z", flip) for flip in (2, 3, 1))
    even, low = z % 2 == 0, z < 2
    own = jnp.concatenate([jnp.where(even, v, near), jnp.where(even, near, v)], axis=axis)
    other = jnp.concatenate([jnp.where(even, far, wrap), jnp.where(even, wrap, far)], axis=axis)
    return jnp.concatenate([jnp.where(low, own, other), jnp.where(low, other, own)], axis=axis)


def norms(points):
    wide = points.astype(jnp.float32)
    return jnp.sum(wide * wide, axis=0)


def per_device(source, target, source_logw, target_logw, start_potential):
    z, y, xh, xl, core = (lax.axis_index(name) for name in names)
    width, span = source.shape[1], target.shape[1]

    sources = source[None]
    targets = jnp.concatenate([target, start_potential], axis=0)[None]
    other = exchange(sources, "core", 1)
    sources = jnp.zeros((2, dim, width), sources.dtype)
    sources = lax.dynamic_update_slice(sources, source[None], (core, 0, 0))
    sources = lax.dynamic_update_slice(sources, other, (1 - core, 0, 0))
    sources = doubled(sources, x, 1, xl)
    direct = [exchange(targets, axes, flip) for axes, flip in ((x, 3), ("y", 3), (("y", *x), 15))]
    targets = jnp.concatenate([targets, *direct], axis=0)
    sources = all_along_z(sources, z, 0)
    others = exchange(targets, "y", 1)

    lse, held, shift, biases = first_row_sums(targets, sources)
    lse, other_biases = next_row_sums(others, lse, held, shift)
    column_base = smoothing * target_logw
    lse, column_base = lax.optimization_barrier((lse, column_base))
    count = lse.shape[1]
    logw = source_logw[None]
    received = [exchange(jnp.concatenate([lse, logw], axis=1), "z", flip) for flip in (2, 3, 1)]
    parts = [v[:, :count] for v in received]
    lse = log_add(log_add(lse, parts[0]), log_add(parts[1], parts[2]))
    far, wrap, near = (v[:, count:] for v in received)
    even, low = z % 2 == 0, z < 2
    own = jnp.concatenate([jnp.where(even, logw, near), jnp.where(even, near, logw)], axis=1)
    other = jnp.concatenate([jnp.where(even, far, wrap), jnp.where(even, wrap, far)], axis=1)
    logw = jnp.where(
        low, jnp.concatenate([own, other], axis=1), jnp.concatenate([other, own], axis=1)
    )
    beside = exchange(lse, x, 1)
    across = exchange(lse, (*x, "core"), 3)
    lse = log_add(lse, exchange(lse, "core", 1))
    partial, stream = first_column_sums(others, other_biases, sources, lse, beside, across, logw)
    sent = exchange(partial, "y", 1)
    half = 2 * span
    partial = next_column_sums(stream, targets, biases, 2, 2)
    partial = log_add(partial, sent[:, half:])
    more = exchange(partial, "y", 3)
    partial = next_column_sums(stream, targets, biases, 1, 1)
    partial = log_add(log_add(partial, sent[:, span:half]), more[:, span:])

    at = z
    lse = log_add(lse, log_add(beside, across))
    mine = lax.dynamic_index_in_dim(lse.reshape(4, 4 * width), at, 0, False)
    picked = lax.dynamic_index_in_dim(sources.reshape(4, 4, dim, width), at, 0, False)
    row_sq = jnp.sum(jnp.square(picked.astype(jnp.float32)), axis=1).reshape(4 * width)
    row_lse = mine / log2e - row_sq / smoothing
    row_potential = smoothing * source_logw - smoothing * row_lse
    partial, row_potential = lax.optimization_barrier((partial, row_potential))
    last = exchange(partial, x, 3)
    partial = next_column_sums(stream, targets, biases, 0, 1)
    partial = log_add(log_add(partial, sent[:, :span]), more[:, :span])
    partial = log_add(partial, last)[0]

    col_lse = partial / log2e - norms(target) / smoothing
    col_potential = column_base - smoothing * col_lse
    return (row_potential, col_potential)


def solution(mesh):
    devices = Mesh(mesh.devices.reshape(shape), names)
    rows = ("z", "y", "xh")
    columns_over = ("xl", "core", "z", "y", "xh")
    in_specs = (P(None, names), P(None, columns_over), P(rows), P(columns_over), P(None, columns_over))
    out_specs = (P(rows), P(columns_over))
    return jax.shard_map(
        per_device, mesh=devices, in_specs=in_specs, out_specs=out_specs, check_vma=False
    )
```

```python
import functools
import math

import jax
import jax.numpy as jnp
from jax import lax
from jax.experimental import pallas as pl
from jax.experimental.pallas import tpu as pltpu
from jax.sharding import Mesh
from jax.sharding import PartitionSpec as P

smoothing = 0.1
log2e = math.log2(math.e)
kappa = 2.0 * log2e / smoothing
scale = log2e / smoothing
dim = 64
headroom = 48.0
sample = 32
redo_chunk = 256
row_blocks = (1024, 1024)
column_blocks = (1024, 768)
largest = 3e38
smallest = 2.0**-90
shape = (4, 4, 2, 2, 2)
names = ("z", "y", "xh", "xl", "core")
x = ("xh", "xl")
along_z = (0, 1, 2, 3)


def three_parts(v):
    hi = v.astype(jnp.bfloat16).astype(jnp.float32)
    mid = (v - hi).astype(jnp.bfloat16).astype(jnp.float32)
    return hi, mid, v - hi - mid


def rounded(v):
    return v.astype(jnp.bfloat16).astype(jnp.float32)


def log_add(a, b):
    top = jnp.maximum(a, b)
    return top + jnp.log2(1.0 + jnp.exp2(-jnp.abs(a - b)))


def streamed_features(points, bias):
    m = points.shape[1]
    hi, mid, lo = three_parts(bias)
    row = lax.broadcasted_iota(jnp.int32, (16, m), 0)
    extra = jnp.where(row == 0, hi, jnp.where(row == 1, mid, jnp.where(row == 2, lo, 0.0)))
    extra = jnp.where(row == 3, 1.0, extra).astype(jnp.bfloat16)
    block = jnp.concatenate([points, extra, jnp.zeros((48, m), jnp.bfloat16)], axis=0)
    return block.T


def fill_held(held_ref, start, points):
    cols = slice(start, start + points.shape[1])
    wide = points.astype(jnp.float32) * kappa
    hi = wide.astype(jnp.bfloat16)
    held_ref[:dim, cols] = hi
    held_ref[dim:, cols] = (wide - hi.astype(jnp.float32)).astype(jnp.bfloat16)


class LogSums:
    def __init__(self, stream_ref, held_ref, extra_ref, out_ref, shift_ref, blocks):
        self.stream_ref, self.held_ref, self.extra_ref = stream_ref, held_ref, extra_ref
        self.out_ref, self.shift_ref = out_ref, shift_ref
        self.chunk, self.tile = blocks
        self.m, self.n = stream_ref.shape[0], held_ref.shape[1]
        self.unroll = 2 if self.n // self.tile % 2 == 0 and self.n > 2000 else 1

    def scores(self, start, size, cols):
        u = self.stream_ref[pl.ds(start, size), :]
        held = self.held_ref[:, cols]
        zeros = jnp.zeros((dim, held.shape[1]), jnp.bfloat16)
        held = jnp.concatenate(
            [held[:dim], self.extra_ref[:, cols], zeros[:48], held[dim:], zeros], axis=0
        )
        return lax.dot_general(
            jnp.concatenate([u, u], axis=1),
            held,
            (((1,), (0,)), ((), ())),
            preferred_element_type=jnp.float32,
        )

    def set_extra(self, shift):
        row = lax.broadcasted_iota(jnp.int32, (16, self.n), 0)
        extra = jnp.where(row < 3, 1.0, jnp.where(row == 3, -shift, 0.0))
        self.extra_ref[...] = extra.astype(jnp.bfloat16)

    def tiles(self, step):
        def body(t, _):
            step(pl.ds(pl.multiple_of(t * self.tile, self.tile), self.tile))
            return 0

        lax.fori_loop(0, self.n // self.tile, body, 0, unroll=self.unroll)

    def estimate(self):
        self.set_extra(jnp.zeros((1, self.n), jnp.float32))
        top = jnp.max(self.scores(0, sample, slice(None)), axis=0, keepdims=True)
        self.shift_ref[...] = rounded(top + headroom)

    def sums(self):
        self.set_extra(self.shift_ref[...])

        def add_up(cols):
            acc = jnp.zeros((8, self.tile), jnp.float32)
            for c in range(self.m // self.chunk):
                e = jnp.exp2(self.scores(c * self.chunk, self.chunk, cols))
                acc = acc + jnp.sum(e.reshape(self.chunk // 8, 8, self.tile), axis=0)
            self.out_ref[:, cols] = jnp.sum(acc, axis=0, keepdims=True)

        self.tiles(add_up)
        return self.out_ref[...]

    def exact(self):
        self.set_extra(jnp.zeros((1, self.n), jnp.float32))

        def highest(cols):
            def step(c, acc):
                v = self.scores(pl.multiple_of(c * redo_chunk, redo_chunk), redo_chunk, cols)
                return jnp.maximum(acc, jnp.max(v, axis=0, keepdims=True))

            none = jnp.full((1, self.tile), -largest, jnp.float32)
            self.out_ref[:, cols] = lax.fori_loop(0, self.m // redo_chunk, step, none)

        self.tiles(highest)
        return self.out_ref[...]

    def run(self, prior=None):
        def attempt(state):
            total = self.sums()
            if prior is not None:
                total = total + jnp.exp2(prior - self.shift_ref[...])
            in_range = jnp.logical_and(jnp.max(total) < largest, jnp.min(total) > smallest)
            again = jnp.logical_not(in_range)
            self.out_ref[...] = self.shift_ref[...] + jnp.log2(total)

            @pl.when(again)
            def _():
                top = self.exact()
                self.shift_ref[...] = rounded(top if prior is None else jnp.maximum(top, prior))

            return state[0] + 1, again

        lax.while_loop(lambda s: jnp.logical_and(s[1], s[0] < 2), attempt, (0, True))


def fill_row_stream(t_ref, stream_ref, bias_ref):
    pieces, _, width = t_ref.shape
    for k in range(pieces):
        points = t_ref[k, :dim, :]
        lifted = t_ref[k, dim : dim + 1, :].astype(jnp.float32)
        wide = points.astype(jnp.float32)
        bias = scale * (lifted - jnp.sum(wide * wide, axis=0, keepdims=True))
        bias_ref[:, k * width : (k + 1) * width] = bias
        stream_ref[k * width : (k + 1) * width, :] = streamed_features(points, bias)


def first_row_kernel(t_ref, s_ref, out_ref, held_ref, shift_ref, bias_ref, stream_ref, extra_ref):
    fill_row_stream(t_ref, stream_ref, bias_ref)
    for k in range(s_ref.shape[0]):
        fill_held(held_ref, k * s_ref.shape[2], s_ref[k, :dim, :])
    sums = LogSums(stream_ref, held_ref, extra_ref, out_ref, shift_ref, row_blocks)
    sums.estimate()
    sums.run()


def next_row_kernel(
    t_ref, held_ref, old_ref, prior_ref, out_ref, bias_ref, stream_ref, extra_ref, shift_ref
):
    fill_row_stream(t_ref, stream_ref, bias_ref)
    shift_ref[...] = old_ref[...]
    LogSums(stream_ref, held_ref, extra_ref, out_ref, shift_ref, row_blocks).run(prior_ref[...])


def fill_column_stream(s_ref, lse_ref, near_ref, far_ref, logw_ref, stream_ref):
    pieces, _, width = s_ref.shape
    per = pieces // len(along_z)
    for k in range(pieces):
        at = (along_z[k // per] * per + k % per) * width
        cols = slice(k * width, (k + 1) * width)
        lse = log_add(lse_ref[:, cols], log_add(near_ref[:, cols], far_ref[:, cols]))
        bias = log2e * logw_ref[:, at : at + width] - lse
        stream_ref[cols, :] = streamed_features(s_ref[k], bias)


def columns(first, t_ref, bias_ref, out_ref, stream_ref, held_ref, extra_ref, shift_ref):
    width = t_ref.shape[2]
    start = first * width
    shift_ref[...] = rounded(-bias_ref[:, start : start + held_ref.shape[1]])
    for k in range(held_ref.shape[1] // width):
        fill_held(held_ref, k * width, t_ref[first + k, :dim, :])
    LogSums(stream_ref, held_ref, extra_ref, out_ref, shift_ref, column_blocks).run()


def first_column_kernel(*refs):
    ins, (t_ref, bias_ref, out_ref, stream_ref), scratch = refs[:-7], refs[-7:-3], refs[-3:]
    fill_column_stream(*ins, stream_ref)
    columns(0, t_ref, bias_ref, out_ref, stream_ref, *scratch)


def next_column_kernel(first, stream_ref, t_ref, bias_ref, out_ref, *scratch):
    columns(first, t_ref, bias_ref, out_ref, stream_ref, *scratch)


whole = pl.BlockSpec(memory_space=pltpu.VMEM)


def call(kernel, name, operands, outs, scratch):
    return pl.pallas_call(
        kernel,
        in_specs=[whole] * len(operands),
        out_specs=[whole] * len(outs),
        out_shape=[jax.ShapeDtypeStruct(*o) for o in outs],
        scratch_shapes=[pltpu.VMEM(*s) for s in scratch],
        compiler_params=pltpu.CompilerParams(vmem_limit_bytes=40 * 2**20),
        name=name,
    )(*operands)


def stream_of(points):
    return ((points, 128), jnp.bfloat16)


def arrays_of(n):
    row = ((1, n), jnp.float32)
    return row, ((2 * dim, n), jnp.bfloat16), ((16, n), jnp.bfloat16)


def points_of(targets):
    return targets.shape[0] * targets.shape[2]


def first_row_sums(targets, sources):
    row, held, extra = arrays_of(points_of(sources))
    outs = (row, held, row, arrays_of(points_of(targets))[0])
    scratch = (stream_of(points_of(targets)), extra)
    return call(first_row_kernel, "first_row_sums", (targets, sources), outs, scratch)


def next_row_sums(targets, prior, held, shift):
    row, _, extra = arrays_of(held.shape[1])
    outs = (row, arrays_of(points_of(targets))[0])
    scratch = (stream_of(points_of(targets)), extra, row)
    return call(next_row_kernel, "next_row_sums", (targets, held, shift, prior), outs, scratch)


def first_column_sums(targets, biases, sources, *more):
    row, held, extra = arrays_of(points_of(targets))
    operands = (sources, *more, targets, biases)
    outs = (row, stream_of(points_of(sources)))
    return call(first_column_kernel, "first_column_sums", operands, outs, (held, extra, row))


def next_column_sums(stream, targets, biases, first, count):
    row, held, extra = arrays_of(count * targets.shape[2])
    kernel = functools.partial(next_column_kernel, first)
    operands = (stream, targets, biases)
    return call(kernel, "next_column_sums", operands, (row,), (held, extra, row))[0]


def exchange(v, axes, flip):
    size = lax.axis_size(axes)
    return lax.ppermute(v, axes, [(i, i ^ flip) for i in range(size)])


def in_order(bit, v, other):
    first = bit == 0
    return jnp.concatenate([jnp.where(first, v, other), jnp.where(first, other, v)], axis=0)


def doubled(v, axes, flip, bit):
    return in_order(bit, v, exchange(v, axes, flip))


def all_along_z(v, z, axis):
    far, wrap, near = (exchange(v, "z", flip) for flip in (2, 3, 1))
    even, low = z % 2 == 0, z < 2
    own = jnp.concatenate([jnp.where(even, v, near), jnp.where(even, near, v)], axis=axis)
    other = jnp.concatenate([jnp.where(even, far, wrap), jnp.where(even, wrap, far)], axis=axis)
    return jnp.concatenate([jnp.where(low, own, other), jnp.where(low, other, own)], axis=axis)


def norms(points):
    wide = points.astype(jnp.float32)
    return jnp.sum(wide * wide, axis=0)


def per_device(source, target, source_logw, target_logw, start_potential):
    z, y, xh, xl, core = (lax.axis_index(name) for name in names)
    width, span = source.shape[1], target.shape[1]

    sources = source[None]
    targets = jnp.concatenate([target, start_potential], axis=0)[None]
    beside = exchange(sources, x, 1)
    across = exchange(sources, (*x, "core"), 3)
    other = exchange(sources, "core", 1)
    sources = jnp.zeros((4, dim, width), sources.dtype)
    sources = lax.dynamic_update_slice(sources, source[None], (2 * xl + core, 0, 0))
    sources = lax.dynamic_update_slice(sources, other, (2 * xl + 1 - core, 0, 0))
    sources = lax.dynamic_update_slice(sources, beside, (2 - 2 * xl + core, 0, 0))
    sources = lax.dynamic_update_slice(sources, across, (3 - 2 * xl - core, 0, 0))
    direct = [exchange(targets, axes, flip) for axes, flip in ((x, 3), ("y", 3), (("y", *x), 15))]
    targets = jnp.concatenate([targets, *direct], axis=0)
    sources = all_along_z(sources, z, 0)
    others = exchange(targets, "y", 1)

    lse, held, shift, biases = first_row_sums(targets, sources)
    lse, other_biases = next_row_sums(others, lse, held, shift)
    column_base = smoothing * target_logw
    lse, column_base = lax.optimization_barrier((lse, column_base))
    count = lse.shape[1]
    logw = source_logw[None]
    received = [exchange(jnp.concatenate([lse, logw], axis=1), "z", flip) for flip in (2, 3, 1)]
    parts = [v[:, :count] for v in received]
    lse = log_add(log_add(lse, parts[0]), log_add(parts[1], parts[2]))
    far, wrap, near = (v[:, count:] for v in received)
    even, low = z % 2 == 0, z < 2
    own = jnp.concatenate([jnp.where(even, logw, near), jnp.where(even, near, logw)], axis=1)
    other = jnp.concatenate([jnp.where(even, far, wrap), jnp.where(even, wrap, far)], axis=1)
    logw = jnp.where(
        low, jnp.concatenate([own, other], axis=1), jnp.concatenate([other, own], axis=1)
    )
    beside = exchange(lse, x, 1)
    across = exchange(lse, (*x, "core"), 3)
    lse = log_add(lse, exchange(lse, "core", 1))
    partial, stream = first_column_sums(others, other_biases, sources, lse, beside, across, logw)
    sent = exchange(partial, "y", 1)
    half = 2 * span
    partial = next_column_sums(stream, targets, biases, 2, 2)
    partial = log_add(partial, sent[:, half:])
    more = exchange(partial, "y", 3)
    partial = next_column_sums(stream, targets, biases, 1, 1)
    partial = log_add(log_add(partial, sent[:, span:half]), more[:, span:])

    at = z
    lse = log_add(lse, log_add(beside, across))
    mine = lax.dynamic_index_in_dim(lse.reshape(4, 4 * width), at, 0, False)
    picked = lax.dynamic_index_in_dim(sources.reshape(4, 4, dim, width), at, 0, False)
    row_sq = jnp.sum(jnp.square(picked.astype(jnp.float32)), axis=1).reshape(4 * width)
    row_lse = mine / log2e - row_sq / smoothing
    row_potential = smoothing * source_logw - smoothing * row_lse
    partial, row_potential = lax.optimization_barrier((partial, row_potential))
    last = exchange(partial, x, 3)
    partial = next_column_sums(stream, targets, biases, 0, 1)
    partial = log_add(log_add(partial, sent[:, :span]), more[:, :span])
    partial = log_add(partial, last)[0]

    col_lse = partial / log2e - norms(target) / smoothing
    col_potential = column_base - smoothing * col_lse
    return (row_potential, col_potential)


def solution(mesh):
    devices = Mesh(mesh.devices.reshape(shape), names)
    rows = ("z", "y", "xh")
    columns_over = ("xl", "core", "z", "y", "xh")
    in_specs = (P(None, names), P(None, columns_over), P(rows), P(columns_over), P(None, columns_over))
    out_specs = (P(rows), P(columns_over))
    return jax.shard_map(
        per_device, mesh=devices, in_specs=in_specs, out_specs=out_specs, check_vma=False
    )
```
